128 devices in a mesh: gx: 8 (over x, core), gy: 16 (over y, z).
Axes of the slice: x: 4, y: 4, z: 4, core: 2. Of those that a mesh axis runs over, the one named last changes fastest.
Arguments:
- atm_blocks: bfloat16 [16384, 30, 256], P(('gx', 'gy')), may hold values from -6 to 6
- tile_dev: int32 [32768, 1], replicated, may hold values from 0 to 127; in each aligned block of 256 rows (0 to 255, 256 to 511, ...) at most 3 rows name the same one
- tile_blk: int32 [32768], replicated, may hold values from 0 to 127
- tile_weights: bfloat16 [32768, 256, 128], P(('gx', 'gy')), may hold values from -0.375 to 0.375
- tile_dst: int32 [32768], P(('gx', 'gy')), may hold values from 0 to 63
- ocean_frac: float32 [8192, 128], P(('gx', 'gy')), may hold values from 0.5 to 1
- halo_send: int32 [128, 2, 8], P(('gx', 'gy')), may hold values from 0 to 63
Outputs:
- ocean_fields: bfloat16 [8192, 30, 128], P(('gx', 'gy'))
- ocean_halo: bfloat16 [128, 2, 8, 30, 128], P(('gx', 'gy'))
The draws below stay inside these ranges and needn't reach their ends.
Inputs may be any that keep to these rules, and one draw needn't show every extreme that they name: `tile_dev`: within the 256 rows of one device (aligned blocks of rows), no source device is named more than 3 times, and some source device is named exactly 3 times.
All inputs are finite; a program needn't handle non-finite values.
Results may differ from the reference program's by a relative error of at most 0.001.
Values may be sent and summed in bfloat16 or wider, within the bound.
A program may use at most 128 MiB of HBM per device.

```python
import math
import jax
import jax.numpy as jnp
import numpy as np
from jax import lax

F = 30
NP = 256
TC = 128
BA = 128
TILE_DEV = 256
OB = 64
HB = 8
CAP = 3
BLOCKS_A = 16384
TILES = 32768
OCEAN_BLOCKS = 8192
DEVICES = 128


def touch_ends(drawn, rng, smallest, largest):
    longest = drawn.shape.index(max(drawn.shape))
    spots = []
    for shift in (0, 1):
        where = [jax.random.randint(jax.random.fold_in(rng, axis), (), 0, length) for axis, length in enumerate(drawn.shape)]
        where[longest] = (where[longest] + shift) % drawn.shape[longest]
        spots.append(tuple(where))
    return drawn.at[spots[0]].set(smallest).at[spots[1]].set(largest)


def shard_levels(rng, extent, split, smallest, high):
    def one(dim, blocks):
        steps = jax.random.uniform(jax.random.fold_in(jax.random.fold_in(rng, 6), dim), (blocks,), jnp.float32, smallest / len(split), high / len(split))
        return jnp.repeat(jnp.exp(steps), extent[dim] // blocks).reshape((-1,) + (1,) * (len(extent) - dim - 1))

    gain = one(*split[0])
    for cut in split[1:]:
        gain = gain * one(*cut)
    return gain


def shared_out(own_key, own, number, rows, amount, top, limit, skew):
    sequence = jax.random.permutation(own_key, amount)
    heavy_load, ordinary = portions_of(amount, rows * top, limit, skew, True), portions_of(amount, rows * top, limit, skew, False)
    places = jnp.arange(amount)

    def named(sizes, rotation):
        used = int((sizes > 0).sum())
        fixed = max(1, used // 4)
        moved = fixed + (places - fixed + rotation * (used - fixed)) % max(1, amount - fixed)
        return jnp.zeros((amount,), jnp.int32).at[sequence[jnp.where(places < fixed, places, moved)]].set(jnp.asarray(sizes, jnp.int32))

    sizes = jnp.where(number % 4 == 0, named(heavy_load, number // 4), named(ordinary, number - number // 4 - 1))
    mixed = jax.random.permutation(jax.random.fold_in(own, 3), amount)
    giver, sink = mixed[0:amount // 2 * 2:2], mixed[1:amount // 2 * 2:2]
    slack = jnp.minimum(sizes[giver] - 1, limit - sizes[sink]) // 2
    slack = jnp.where((giver == sequence[0]) | (sink == sequence[0]) | (sizes[sink] == 0), 0, jnp.maximum(slack, 0))
    moved = jax.random.randint(jax.random.fold_in(own, 4), (amount // 2,), 0, 1 << 20) % (slack + 1)
    sizes = sizes.at[giver].add(-moved).at[sink].add(moved)
    items = jnp.searchsorted(jnp.cumsum(sizes), jnp.arange(rows * top), side="right").astype(jnp.int32)
    listing = items.reshape(top, rows).T
    listing = listing[jax.random.permutation(jax.random.fold_in(own, 1), rows)]
    rotation = jax.random.randint(jax.random.fold_in(own, 2), (rows, 1), 0, top)
    return jnp.take_along_axis(listing, (jnp.arange(top)[None, :] + rotation) % top, axis=1)


def portions_of(amount, total, limit, skew, full):
    portions = [(1 << 20) // math.isqrt(standing ** skew) + 1 for standing in range(1, amount + 1)]
    largest = limit if full else min(limit, max(-(-total // amount), total * portions[0] // sum(portions)))
    least = 1 if total - largest >= amount - 1 else 0
    holding, surplus = [largest] + [least] * (amount - 1), total - largest - least * (amount - 1)
    while surplus > 0:
        movable = [i for i in range(1, amount) if holding[i] < largest] or [i for i in range(1, amount) if holding[i] < limit]
        pool, left = sum([portions[i] for i in movable]), surplus
        for i in movable:
            addition = min(limit - holding[i], max(1, left * portions[i] // pool), surplus)
            holding[i] = holding[i] + addition
            surplus = surplus - addition
    return np.array(holding)


def bell_draw(own_key, shape, width, most, split=(), held_as=jnp.bfloat16):
    drawn = jax.random.normal(own_key, shape, jnp.float32) * width
    if len(split) > 0:
        drawn = shard_levels(own_key, shape, split, -0.22, 0.18) * drawn
    return jnp.clip(drawn, min=-most, max=most).astype(held_as)


def setup_inputs(seed: int = 0) -> dict:
    arg_keys = jax.random.split(jax.random.key(seed), 8)
    atm_blocks = bell_draw(arg_keys[0], (BLOCKS_A, F, NP), 1.0, 6.0, ((0, 128),))
    tile_dev_keys = jax.random.split(jax.random.fold_in(arg_keys[1], 1), TILES // TILE_DEV)
    tile_dev_turns = jax.random.permutation(jax.random.fold_in(arg_keys[1], 3), TILES // TILE_DEV)
    tile_dev = jax.vmap(lambda own, number: shared_out(jax.random.fold_in(arg_keys[1], 2), own, number, TILE_DEV, DEVICES, 1, CAP, 1))(tile_dev_keys, tile_dev_turns).reshape((TILES, 1))
    tile_blk = touch_ends(jax.random.randint(arg_keys[2], (TILES,), 0, BA), jax.random.fold_in(arg_keys[2], 1), 0, BA - 1).astype(jnp.int32)
    tile_weights = bell_draw(arg_keys[3], (TILES, NP, TC), NP ** -0.5, 0.375, ((0, 128),))
    tile_dst = touch_ends(jax.random.randint(arg_keys[4], (TILES,), 0, OB), jax.random.fold_in(arg_keys[4], 1), 0, OB - 1).astype(jnp.int32)
    ocean_frac = jnp.clip(0.5 + 0.5 * jax.random.uniform(arg_keys[5], (OCEAN_BLOCKS, TC), jnp.float32) ** shard_levels(arg_keys[5], (OCEAN_BLOCKS, TC), ((0, 128),), -0.2, 0.2), 0.5, 1.0)
    halo_send = touch_ends(jax.random.randint(arg_keys[6], (DEVICES, 2, HB), 0, OB), jax.random.fold_in(arg_keys[6], 1), 0, OB - 1).astype(jnp.int32)
    return {"atm_blocks": atm_blocks, "tile_dev": tile_dev, "tile_blk": tile_blk, "tile_weights": tile_weights, "tile_dst": tile_dst, "ocean_frac": ocean_frac, "halo_send": halo_send}


def reference(atm_blocks, tile_dev, tile_blk, tile_weights, tile_dst, ocean_frac, halo_send):
    flat_index = (tile_dev[:, 0] * BA + tile_blk).astype(jnp.int32).reshape(DEVICES, TILE_DEV)
    weights = tile_weights.reshape(DEVICES, TILE_DEV, NP, TC)
    targets = tile_dst.reshape(DEVICES, TILE_DEV)
    fractions = ocean_frac.reshape(DEVICES, OB, TC)

    def one_device(packed):
        index_list, weight_tiles, target_list, frac_rows = packed
        gathered = atm_blocks[index_list].astype(jnp.float32)
        results = jnp.einsum("tfk,tkc->tfc", gathered, weight_tiles.astype(jnp.float32))
        onehot = (target_list[None, :] == jnp.arange(OB, dtype=jnp.int32)[:, None]).astype(jnp.float32)
        totals = jnp.dot(onehot, results.reshape(TILE_DEV, F * TC), precision=lax.Precision.HIGHEST)
        return (totals.reshape(OB, F, TC) / frac_rows[:, None, :]).astype(jnp.bfloat16)

    fields = lax.map(one_device, (flat_index, weights, targets, fractions))
    devices_idx = jnp.arange(DEVICES, dtype=jnp.int32)
    lower_dev = (devices_idx - 1) % DEVICES
    upper_dev = (devices_idx + 1) % DEVICES

    def pick(device_id, list_row):
        return fields[device_id][list_row]

    from_lower = jax.vmap(pick)(lower_dev, halo_send[lower_dev, 1])
    from_upper = jax.vmap(pick)(upper_dev, halo_send[upper_dev, 0])
    ocean_halo = jnp.stack([from_lower, from_upper], axis=1)
    return fields.reshape(OCEAN_BLOCKS, F, TC), ocean_halo
```

```python
import functools

import jax
import jax.numpy as jnp
from jax import lax
from jax.experimental import pallas as pl
from jax.experimental.pallas import tpu as pltpu
from jax.sharding import PartitionSpec as P

MESH = pl.DeviceIdType.MESH
DEVICES = 128
CAP = 3
GROUP = 21
GROUPS = 6


def step_offset(i):
    j = jnp.where(i < 126, lax.rem(i * 37, 126) + 2, 1)
    return j // 32, lax.rem(j // 8, 4), lax.rem(j // 2, 4), lax.rem(j, 2)


def exchange_kernel(
    send_blk, tile_of, seg_slot, seg_keep, seg_last, halo_idx,
    atm, weights, frac, out_hbm, halo_hbm,
    outgoing, incoming, near, w_vmem, results, running, fields, rim,
    send_sem, recv_sem, near_sem, w_sem, rim_send, rim_recv, out_sem,
):
    gx, gy = lax.axis_index("gx"), lax.axis_index("gy")
    myself = gx * 16 + gy
    x, c, y, z = gx // 2, lax.rem(gx, 2), gy // 4, lax.rem(gy, 4)

    def target(i):
        dx, dy, dz, dc = step_offset(i)
        return lax.rem(x + dx, 4) * 2 + lax.rem(c + dc, 2), lax.rem(y + dy, 4) * 4 + lax.rem(z + dz, 4)

    def source(i):
        dx, dy, dz, dc = step_offset(i)
        gx_s = lax.rem(x - dx + 4, 4) * 2 + lax.rem(c + dc, 2)
        return gx_s * 16 + lax.rem(y - dy + 4, 4) * 4 + lax.rem(z - dz + 4, 4)

    barrier = pltpu.get_barrier_semaphore()

    @pl.loop(0, DEVICES - 1)
    def _(i):
        pl.semaphore_signal(barrier, inc=1, device_id=target(i), device_id_type=MESH)

    w_copy = pltpu.make_async_copy(weights, w_vmem, w_sem)
    w_copy.start()

    def pack(buffer, slot, d):
        for k in range(CAP):
            buffer[slot * CAP + k] = atm[send_blk[d * CAP + k]]

    pack(near, 1, myself)
    pl.semaphore_wait(barrier, DEVICES - 1)

    for g in range(GROUPS):

        @pl.loop(0, GROUP)
        def _(j, g=g):
            i = g * GROUP + j
            dgx, dgy = target(i)
            pack(outgoing, i, dgx * 16 + dgy)
            pltpu.make_async_remote_copy(
                src_ref=outgoing.at[pl.ds(i * CAP, CAP)],
                dst_ref=incoming[g].at[pl.ds(j * CAP, CAP)],
                send_sem=send_sem,
                recv_sem=recv_sem.at[g],
                device_id=(dgx, dgy),
                device_id_type=MESH,
            ).start()

    last = DEVICES - 2
    dgx, dgy = target(last)
    pack(outgoing, last, dgx * 16 + dgy)
    near_copy = pltpu.make_async_remote_copy(
        src_ref=outgoing.at[pl.ds(last * CAP, CAP)],
        dst_ref=near.at[pl.ds(0, CAP)],
        send_sem=near_sem.at[0],
        recv_sem=near_sem.at[1],
        device_id=(dgx, dgy),
        device_id_type=MESH,
    )
    near_copy.start()
    w_copy.wait()

    def multiply(buffer, slot, s):
        for k in range(CAP):
            results[s * CAP + k] = jnp.dot(
                buffer[slot * CAP + k], w_vmem[tile_of[s * CAP + k]], preferred_element_type=jnp.float32
            )

    multiply(near, 1, myself)
    near_copy.wait()
    multiply(near, 0, source(last))
    for g in range(GROUPS):
        pltpu.make_async_copy(incoming[g], incoming[g], recv_sem.at[g]).wait()

        @pl.loop(0, GROUP)
        def _(j, g=g):
            multiply(incoming[g], j, source(g * GROUP + j))

    tiles = running.shape[0]

    def add(r, total):
        total = total * seg_keep[r].astype(jnp.float32) + results[seg_slot[r]]
        running[r] = total
        return total

    lax.fori_loop(0, tiles, add, jnp.zeros(running.shape[1:], jnp.float32))

    @pl.loop(0, fields.shape[0])
    def _(b):
        end = seg_last[b]
        total = jnp.where(end >= 0, running[jnp.maximum(end, 0)], 0.0)
        fields[b] = (total / frac[pl.ds(b, 1), :]).astype(jnp.bfloat16)

    out_copy = pltpu.make_async_copy(fields, out_hbm, out_sem)
    out_copy.start()
    rim_n = rim.shape[0] // 2
    for j in range(2 * rim_n):
        rim[j] = fields[halo_idx[j]]
    up, down = lax.rem(myself + 1, DEVICES), lax.rem(myself + DEVICES - 1, DEVICES)
    rim_copies = []
    for side, there in ((1, up), (0, down)):
        copy = pltpu.make_async_remote_copy(
            src_ref=rim.at[pl.ds(side * rim_n, rim_n)],
            dst_ref=halo_hbm.at[1 - side],
            send_sem=rim_send.at[side],
            recv_sem=rim_recv.at[side],
            device_id=(there // 16, lax.rem(there, 16)),
            device_id_type=MESH,
        )
        copy.start()
        rim_copies.append(copy)
    for copy in rim_copies:
        copy.wait()
    out_copy.wait()
    body = outgoing.at[pl.ds(0, (DEVICES - 2) * CAP)]
    pltpu.make_async_copy(body, body, send_sem).wait()


def per_device(atm_blocks, tile_dev, tile_blk, tile_weights, tile_dst, ocean_frac, halo_send):
    myself = lax.axis_index(("gx", "gy"))
    tiles, nodes, cells = tile_weights.shape
    fields_n = atm_blocks.shape[1]
    ocean_n = ocean_frac.shape[0]
    rim_n = halo_send.shape[2]
    source_dev = tile_dev.reshape(DEVICES, tiles)
    block_of = tile_blk.reshape(DEVICES, tiles)
    slots = jnp.arange(CAP, dtype=jnp.int32)
    order = jnp.arange(tiles, dtype=jnp.int32)
    earlier = order[:, None] < order[None, :]
    mine = source_dev == myself
    nth = jnp.dot(mine.astype(jnp.bfloat16), earlier.astype(jnp.bfloat16), preferred_element_type=jnp.float32)
    nth = nth.astype(jnp.int32)
    matched = mine[:, None, :] & (nth[:, None, :] == slots[None, :, None])
    send_blk = jnp.sum(jnp.where(matched, block_of[:, None, :], 0), axis=2).reshape(-1)
    my_source = lax.dynamic_index_in_dim(source_dev, myself, 0, keepdims=False)
    same = (my_source[:, None] == my_source[None, :]) & earlier
    my_nth = jnp.sum(same.astype(jnp.int32), axis=0)
    read_slot = my_source * CAP + my_nth
    slot_range = jnp.arange(DEVICES * CAP, dtype=jnp.int32)
    tile_of = jnp.sum(jnp.where(read_slot[None, :] == slot_range[:, None], order[None, :], 0), axis=1)
    before = (tile_dst[:, None] < tile_dst[None, :]) | ((tile_dst[:, None] == tile_dst[None, :]) & earlier)
    rank = jnp.sum(before.astype(jnp.int32), axis=0)
    placed = rank[None, :] == order[:, None]
    seg_slot = jnp.sum(jnp.where(placed, read_slot[None, :], 0), axis=1)
    seg_dst = jnp.sum(jnp.where(placed, tile_dst[None, :], 0), axis=1)
    seg_keep = jnp.concatenate([jnp.zeros((1,), jnp.int32), (seg_dst[1:] == seg_dst[:-1]).astype(jnp.int32)])
    targets = jnp.arange(ocean_n, dtype=jnp.int32)
    upto = jnp.sum((tile_dst[None, :] <= targets[:, None]).astype(jnp.int32), axis=1)
    any_in = jnp.any(tile_dst[None, :] == targets[:, None], axis=1)
    seg_last = jnp.where(any_in, upto - 1, -1)
    smem = pl.BlockSpec(memory_space=pltpu.SMEM)
    vmem = pl.BlockSpec(memory_space=pltpu.VMEM)
    hbm = pl.BlockSpec(memory_space=pl.ANY)
    block = (fields_n, nodes)
    fields, halo = pl.pallas_call(
        exchange_kernel,
        out_shape=(
            jax.ShapeDtypeStruct((ocean_n, fields_n, cells), jnp.bfloat16),
            jax.ShapeDtypeStruct((2, rim_n, fields_n, cells), jnp.bfloat16),
        ),
        in_specs=[smem] * 6 + [vmem, hbm, vmem],
        out_specs=(hbm, hbm),
        scratch_shapes=[
            pltpu.VMEM(((DEVICES - 1) * CAP,) + block, jnp.bfloat16),
            [pltpu.VMEM((GROUP * CAP,) + block, jnp.bfloat16)] * GROUPS,
            pltpu.VMEM((2 * CAP,) + block, jnp.bfloat16),
            pltpu.VMEM(tile_weights.shape, jnp.bfloat16),
            pltpu.VMEM((DEVICES * CAP, fields_n, cells), jnp.float32),
            pltpu.VMEM((tiles, fields_n, cells), jnp.float32),
            pltpu.VMEM((ocean_n, fields_n, cells), jnp.bfloat16),
            pltpu.VMEM((2 * rim_n, fields_n, cells), jnp.bfloat16),
            pltpu.SemaphoreType.DMA,
            pltpu.SemaphoreType.DMA((GROUPS,)),
            pltpu.SemaphoreType.DMA((2,)),
            pltpu.SemaphoreType.DMA,
            pltpu.SemaphoreType.DMA((2,)),
            pltpu.SemaphoreType.DMA((2,)),
            pltpu.SemaphoreType.DMA,
        ],
        compiler_params=pltpu.CompilerParams(
            collective_id=0, has_side_effects=True, vmem_limit_bytes=56 << 20
        ),
        name="remap_exchange",
    )(
        send_blk, tile_of, seg_slot, seg_keep, seg_last, halo_send.reshape(-1),
        atm_blocks, tile_weights, ocean_frac,
    )
    return fields, halo[None]


def solution(mesh):
    in_specs = (
        P(("gx", "gy"), None, None),
        P(),
        P(),
        P(("gx", "gy"), None, None),
        P(("gx", "gy")),
        P(("gx", "gy"), None),
        P(("gx", "gy"), None, None),
    )
    out_specs = (P(("gx", "gy"), None, None), P(("gx", "gy"), None, None, None, None))
    return jax.shard_map(
        per_device, mesh=mesh, in_specs=in_specs, out_specs=out_specs, check_vma=False
    )
```

```python
import functools

import jax
import jax.numpy as jnp
from jax import lax
from jax.experimental import pallas as pl
from jax.experimental.pallas import tpu as pltpu
from jax.sharding import PartitionSpec as P

MESH = pl.DeviceIdType.MESH
DEVICES = 128
CHIPS = 64
CAP = 3
GROUP = 21
GROUPS = 3
STEPS = GROUP * GROUPS
CORE = 16

SEND, OWN_THIRD, TILE_OF, SEGMENT, UPTO, SHARED = 0, 3, 4, 7, 9, 10
ROWS = 16


def device_index():
    return lax.axis_index("gx") * 16 + lax.axis_index("gy")


def plan_kernel(dev_ref, blk_ref, dst_ref, out_ref):
    n = DEVICES
    myself = device_index()
    lane = lax.broadcasted_iota(jnp.int32, (n, n), 1)
    sub = lax.broadcasted_iota(jnp.int32, (n, n), 0)
    earlier = sub < lane
    halves = [dev_ref[pl.ds(h, n, stride=2), :] for h in (0, 1)]

    full = jnp.zeros((1, n), jnp.int32)
    columns = [half.T for half in halves]
    chips = [((col >> 5) << 4) | (col & 15) for col in columns]
    units = [jnp.left_shift(1, (chip & 7) * 4) for chip in chips]
    for g in range(CHIPS // 8):
        parts = [jnp.where((chip >> 3) == g, unit, 0) for chip, unit in zip(chips, units)]
        counts = jnp.sum(parts[0] + parts[1], axis=0, keepdims=True)
        for j in range(8):
            full = full | (((counts >> (4 * j)) & 15) == 2 * CAP).astype(jnp.int32)
    shared = 1 - jnp.max(full, axis=1, keepdims=True)

    mine = [(half == myself) for half in halves]
    ones = [m.astype(jnp.float32) for m in mine]
    tri = earlier.astype(jnp.bfloat16)
    nth = [jnp.dot(o.astype(jnp.bfloat16), tri, preferred_element_type=jnp.float32) for o in ones]
    first = jnp.sum(ones[0], axis=1, keepdims=True)
    nth[1] = nth[1] + first
    total = first + jnp.sum(ones[1], axis=1, keepdims=True)
    table = jnp.zeros((n, n), jnp.float32)
    for k in range(CAP):
        picked = jnp.zeros((n, 1), jnp.float32)
        for h in (0, 1):
            blocks = blk_ref[pl.ds(h, n, stride=2), :].astype(jnp.float32)
            picked += jnp.sum(jnp.where(mine[h] & (nth[h] == k), blocks, 0.0), axis=1, keepdims=True)
        table = jnp.where(lane == SEND + k, picked, table)
    table = jnp.where(lane == OWN_THIRD, (total >= CAP).astype(jnp.float32), table)
    out_ref[0:8, :] = table.T[0:8, :].astype(jnp.int32)

    def column(row):
        return jnp.broadcast_to(row, (n, n)).T

    src = [dev_ref[pl.ds(2 * myself + h, 1), :] for h in (0, 1)]
    src_col = [column(s) for s in src]

    def count(mask):
        return jnp.sum(mask.astype(jnp.int32), axis=0, keepdims=True)

    place = [
        count((src_col[0] == src[0]) & earlier),
        count(src_col[0] == src[1]) + count((src_col[1] == src[1]) & earlier),
    ]
    slot = []
    for s, p in zip(src, place):
        helper = (s & ~CORE) | (myself & CORE)
        own_chip = (s & ~CORE) == (myself & ~CORE)
        sender = jnp.where((shared == 1) & (p == CAP - 1) & ~own_chip, helper, s)
        slot.append(p * n + sender)
    slot_col = [column(s) for s in slot]
    for k in range(CAP):
        found = jnp.zeros((n, n), jnp.int32)
        for h in (0, 1):
            found += jnp.where(slot_col[h] == lane + k * n, sub + h * n, 0)
        out_ref[TILE_OF + k : TILE_OF + k + 1, :] = jnp.sum(found, axis=0, keepdims=True)

    dst = [dst_ref[h : h + 1, :] for h in (0, 1)]
    key = [d * (2 * n) + lane[0:1] + h * n for h, d in enumerate(dst)]
    key_col = [column(k) for k in key]
    rank = [count(key_col[0] < k) + count(key_col[1] < k) for k in key]
    rank_col = [column(r) for r in rank]
    value_col = [column(s * CHIPS + d) for s, d in zip(slot, dst)]
    for half in (0, 1):
        placed = jnp.zeros((n, n), jnp.int32)
        for h in (0, 1):
            placed += jnp.where(rank_col[h] == lane + half * n, value_col[h], 0)
        out_ref[SEGMENT + half : SEGMENT + half + 1, :] = jnp.sum(placed, axis=0, keepdims=True)
    out_ref[UPTO : UPTO + 1, :] = count(key_col[0] < (lane + 1) * (2 * n)) + count(key_col[1] < (lane + 1) * (2 * n))
    out_ref[SHARED : SHARED + 1, :] = jnp.broadcast_to(shared, (1, n))


def exchange_kernel(
    shared, plan, halo_idx, atm, weights, frac, out_hbm, halo_hbm,
    out_far, out_same, in_far, in_same, lent, borrowed, near, near_out, w_vmem, results, running, fields, rim,
    send_sem, far_sem, same_sem, lend_sem, near_sem, w_sem, rim_send, rim_recv, out_sem,
):
    gx, gy = lax.axis_index("gx"), lax.axis_index("gy")
    myself = gx * 16 + gy
    x, c, y, z = gx // 2, lax.rem(gx, 2), gy // 4, lax.rem(gy, 4)
    other = 1 - c
    far_cap = CAP - 1 if shared else CAP

    def chip_at(i, sign):
        o = lax.rem(i * 37, STEPS) + 1
        cx = lax.rem(x + sign * (o // 16) + 4, 4)
        cy = lax.rem(y + sign * lax.rem(o // 4, 4) + 4, 4)
        cz = lax.rem(z + sign * lax.rem(o, 4) + 4, 4)
        return cx, cy * 4 + cz

    def at(chip, core):
        return chip[0] * 2 + core, chip[1]

    def index(chip, core):
        return chip[0] * 32 + core * 16 + chip[1]

    partner = (x * 2 + other, gy)
    barrier = pltpu.get_barrier_semaphore()
    pl.semaphore_signal(barrier, inc=1, device_id=partner, device_id_type=MESH)

    @pl.loop(0, STEPS)
    def _(i):
        for core in (0, 1):
            pl.semaphore_signal(barrier, inc=1, device_id=at(chip_at(i, 1), core), device_id_type=MESH)

    w_copy = pltpu.make_async_copy(weights, w_vmem, w_sem)
    w_copy.start()

    def block(d, k):
        return atm[plan[SEND + k, d]]

    if shared:

        @pl.loop(0, CHIPS)
        def _(q):
            lent[q] = block(index((q // 16, lax.rem(q, 16)), other), CAP - 1)

    for k in range(CAP):
        near[CAP + k] = block(myself, k)
        near_out[k] = block(index((x, gy), other), k)
    pl.semaphore_wait(barrier, DEVICES - 1)
    if shared:
        lend = pltpu.make_async_remote_copy(
            src_ref=lent, dst_ref=borrowed, send_sem=lend_sem.at[0], recv_sem=lend_sem.at[1],
            device_id=partner, device_id_type=MESH,
        )
        lend.start()
    near_copy = pltpu.make_async_remote_copy(
        src_ref=near_out, dst_ref=near.at[pl.ds(0, CAP)], send_sem=near_sem.at[0], recv_sem=near_sem.at[1],
        device_id=partner, device_id_type=MESH,
    )

    for g in range(GROUPS):

        @pl.loop(0, GROUP)
        def _(j, g=g):
            i = g * GROUP + j
            chip = chip_at(i, 1)
            for k in range(far_cap):
                out_far[i * far_cap + k] = block(index(chip, other), k)
            pltpu.make_async_remote_copy(
                src_ref=out_far.at[pl.ds(i * far_cap, far_cap)],
                dst_ref=in_far[g].at[pl.ds(j * far_cap, far_cap)],
                send_sem=send_sem.at[0], recv_sem=far_sem.at[g],
                device_id=at(chip, other), device_id_type=MESH,
            ).start()

    near_copy.start()
    if shared:
        lend.wait()

    for g in range(GROUPS):

        @pl.loop(0, GROUP)
        def _(j, g=g):
            i = g * GROUP + j
            chip = chip_at(i, 1)
            d = index(chip, c)
            for k in range(far_cap):
                out_same[i * CAP + k] = block(d, k)
            if shared:
                third = block(d, CAP - 1)
                q = chip[0] * 16 + chip[1]
                out_same[i * CAP + CAP - 1] = jnp.where(plan[OWN_THIRD, d] == 1, third, borrowed[q])
            pltpu.make_async_remote_copy(
                src_ref=out_same.at[pl.ds(i * CAP, CAP)],
                dst_ref=in_same[g].at[pl.ds(j * CAP, CAP)],
                send_sem=send_sem.at[1], recv_sem=same_sem.at[g],
                device_id=at(chip, c), device_id_type=MESH,
            ).start()

    w_copy.wait()

    def multiply(buffer, first, s, cap):
        for k in range(cap):
            results[s + DEVICES * k] = jnp.dot(
                buffer[first + k], w_vmem[plan[TILE_OF + k, s]], preferred_element_type=jnp.float32
            )

    multiply(near, CAP, myself, CAP)
    near_copy.wait()
    multiply(near, 0, index((x, gy), other), CAP)
    for buffers, sems, core, cap in ((in_far, far_sem, other, far_cap), (in_same, same_sem, c, CAP)):
        for g in range(GROUPS):
            pltpu.make_async_copy(buffers[g], buffers[g], sems.at[g]).wait()

            @pl.loop(0, GROUP)
            def _(j, g=g, buffers=buffers, core=core, cap=cap):
                multiply(buffers[g], j * cap, index(chip_at(g * GROUP + j, -1), core), cap)

    tiles = running.shape[0]

    def add(r, carry):
        total, previous = carry
        value = plan[SEGMENT + r // DEVICES, lax.rem(r, DEVICES)]
        slot, b = value // CHIPS, lax.rem(value, CHIPS)
        total = total * (b == previous).astype(jnp.float32) + results[slot]
        running[r] = total
        return total, b

    lax.fori_loop(0, tiles, add, (jnp.zeros(running.shape[1:], jnp.float32), jnp.int32(-1)))

    def finish(b, before):
        upto = plan[UPTO, b]
        total = jnp.where(upto > before, running[jnp.maximum(upto - 1, 0)], 0.0)
        fields[b] = (total / frac[pl.ds(b, 1), :]).astype(jnp.bfloat16)
        return upto

    lax.fori_loop(0, fields.shape[0], finish, jnp.int32(0))

    out_copy = pltpu.make_async_copy(fields, out_hbm, out_sem)
    out_copy.start()
    rim_n = rim.shape[0] // 2
    for j in range(2 * rim_n):
        rim[j] = fields[halo_idx[j]]
    up, down = lax.rem(myself + 1, DEVICES), lax.rem(myself + DEVICES - 1, DEVICES)
    rim_copies = []
    for side, there in ((1, up), (0, down)):
        copy = pltpu.make_async_remote_copy(
            src_ref=rim.at[pl.ds(side * rim_n, rim_n)],
            dst_ref=halo_hbm.at[1 - side],
            send_sem=rim_send.at[side],
            recv_sem=rim_recv.at[side],
            device_id=(there // 16, lax.rem(there, 16)),
            device_id_type=MESH,
        )
        copy.start()
        rim_copies.append(copy)
    for copy in rim_copies:
        copy.wait()
    out_copy.wait()
    for which, buffer in enumerate((out_far, out_same)):
        pltpu.make_async_copy(buffer, buffer, send_sem.at[which]).wait()


def exchange(shared, plan, halo_idx, atm, weights, frac):
    tiles, nodes, cells = weights.shape
    fields_n, ocean_n, rim_n = atm.shape[1], frac.shape[0], halo_idx.shape[0] // 2
    smem = pl.BlockSpec(memory_space=pltpu.SMEM)
    vmem = pl.BlockSpec(memory_space=pltpu.VMEM)
    hbm = pl.BlockSpec(memory_space=pl.ANY)
    far_cap = CAP - 1 if shared else CAP
    lent_n = CHIPS if shared else 1

    def blocks(n):
        return pltpu.VMEM((n, fields_n, nodes), jnp.bfloat16)

    return pl.pallas_call(
        functools.partial(exchange_kernel, shared),
        out_shape=(
            jax.ShapeDtypeStruct((ocean_n, fields_n, cells), jnp.bfloat16),
            jax.ShapeDtypeStruct((2, rim_n, fields_n, cells), jnp.bfloat16),
        ),
        in_specs=[smem, smem, vmem, hbm, vmem],
        out_specs=(hbm, hbm),
        scratch_shapes=[
            blocks(STEPS * far_cap),
            blocks(STEPS * CAP),
            [blocks(GROUP * far_cap)] * GROUPS,
            [blocks(GROUP * CAP)] * GROUPS,
            blocks(lent_n),
            blocks(lent_n),
            blocks(2 * CAP),
            blocks(CAP),
            pltpu.VMEM(weights.shape, jnp.bfloat16),
            pltpu.VMEM((DEVICES * CAP, fields_n, cells), jnp.float32),
            pltpu.VMEM((tiles, fields_n, cells), jnp.float32),
            pltpu.VMEM((ocean_n, fields_n, cells), jnp.bfloat16),
            pltpu.VMEM((2 * rim_n, fields_n, cells), jnp.bfloat16),
            pltpu.SemaphoreType.DMA((2,)),
            pltpu.SemaphoreType.DMA((GROUPS,)),
            pltpu.SemaphoreType.DMA((GROUPS,)),
            pltpu.SemaphoreType.DMA((2,)),
            pltpu.SemaphoreType.DMA((2,)),
            pltpu.SemaphoreType.DMA,
            pltpu.SemaphoreType.DMA((2,)),
            pltpu.SemaphoreType.DMA((2,)),
            pltpu.SemaphoreType.DMA,
        ],
        compiler_params=pltpu.CompilerParams(
            collective_id=int(shared), has_side_effects=True, vmem_limit_bytes=56 << 20
        ),
        name="remap_shared" if shared else "remap_direct",
    )(plan, halo_idx, atm, weights, frac)


def per_device(atm_blocks, tile_dev, tile_blk, tile_weights, tile_dst, ocean_frac, halo_send):
    halves = (2 * DEVICES, DEVICES)
    plan = pl.pallas_call(
        plan_kernel,
        out_shape=jax.ShapeDtypeStruct((ROWS, DEVICES), jnp.int32),
        in_specs=[pl.BlockSpec(memory_space=pltpu.VMEM)] * 3,
        out_specs=pl.BlockSpec(memory_space=pltpu.VMEM),
        name="plan",
    )(tile_dev.reshape(halves), tile_blk.reshape(halves), tile_dst.reshape(2, DEVICES))
    fields, halo = lax.cond(
        plan[SHARED, 0] == 1,
        functools.partial(exchange, True),
        functools.partial(exchange, False),
        plan, halo_send.reshape(-1), atm_blocks, tile_weights, ocean_frac,
    )
    return fields, halo[None]


def solution(mesh):
    in_specs = (
        P(("gx", "gy"), None, None),
        P(),
        P(),
        P(("gx", "gy"), None, None),
        P(("gx", "gy")),
        P(("gx", "gy"), None),
        P(("gx", "gy"), None, None),
    )
    out_specs = (P(("gx", "gy"), None, None), P(("gx", "gy"), None, None, None, None))
    return jax.shard_map(
        per_device, mesh=mesh, in_specs=in_specs, out_specs=out_specs, check_vma=False
    )
```

```python
import functools

import jax
import jax.numpy as jnp
from jax import lax
from jax.experimental import pallas as pl
from jax.experimental.pallas import tpu as pltpu
from jax.sharding import PartitionSpec as P

MESH = pl.DeviceIdType.MESH
DEVICES = 128
CHIPS = 64
CAP = 3
STEPS = 63
FAR_GROUPS = (21, 21, 21)
SAME_GROUPS = (21, 21, 14, 7)
CORE = 16

SEND, OWN_THIRD, TILE_OF, SEGMENT, UPTO = 0, 3, 4, 7, 9
ROWS = 16


def device_index():
    return lax.axis_index("gx") * 16 + lax.axis_index("gy")


def plan_kernel(dev_ref, blk_ref, dst_ref, out_ref, shared_ref):
    n = DEVICES
    myself = device_index()
    lane = lax.broadcasted_iota(jnp.int32, (n, n), 1)
    sub = lax.broadcasted_iota(jnp.int32, (n, n), 0)
    earlier = sub < lane
    halves = [dev_ref[pl.ds(h, n, stride=2), :] for h in (0, 1)]

    full = jnp.zeros((1, n), jnp.int32)
    columns = [half.T for half in halves]
    chips = [((col >> 5) << 4) | (col & 15) for col in columns]
    units = [jnp.left_shift(1, (chip & 7) * 4) for chip in chips]
    for g in range(CHIPS // 8):
        parts = [jnp.where((chip >> 3) == g, unit, 0) for chip, unit in zip(chips, units)]
        counts = jnp.sum(parts[0] + parts[1], axis=0, keepdims=True)
        for j in range(8):
            full = full | (((counts >> (4 * j)) & 15) == 2 * CAP).astype(jnp.int32)
    shared = 1 - jnp.max(full, axis=1, keepdims=True)

    mine = [(half == myself) for half in halves]
    ones = [m.astype(jnp.float32) for m in mine]
    tri = earlier.astype(jnp.bfloat16)
    nth = [jnp.dot(o.astype(jnp.bfloat16), tri, preferred_element_type=jnp.float32) for o in ones]
    first = jnp.sum(ones[0], axis=1, keepdims=True)
    nth[1] = nth[1] + first
    total = first + jnp.sum(ones[1], axis=1, keepdims=True)
    table = jnp.zeros((n, n), jnp.float32)
    for k in range(CAP):
        picked = jnp.zeros((n, 1), jnp.float32)
        for h in (0, 1):
            blocks = blk_ref[pl.ds(h, n, stride=2), :].astype(jnp.float32)
            picked += jnp.sum(jnp.where(mine[h] & (nth[h] == k), blocks, 0.0), axis=1, keepdims=True)
        table = jnp.where(lane == SEND + k, picked, table)
    table = jnp.where(lane == OWN_THIRD, (total >= CAP).astype(jnp.float32), table)
    out_ref[0:8, :] = table.T[0:8, :].astype(jnp.int32)

    def column(row):
        return jnp.broadcast_to(row, (n, n)).T

    src = [dev_ref[pl.ds(2 * myself + h, 1), :] for h in (0, 1)]
    src_col = [column(s) for s in src]

    def count(mask):
        return jnp.sum(mask.astype(jnp.int32), axis=0, keepdims=True)

    place = [
        count((src_col[0] == src[0]) & earlier),
        count(src_col[0] == src[1]) + count((src_col[1] == src[1]) & earlier),
    ]
    slot = []
    for s, p in zip(src, place):
        helper = (s & ~CORE) | (myself & CORE)
        own_chip = (s & ~CORE) == (myself & ~CORE)
        sender = jnp.where((shared == 1) & (p == CAP - 1) & ~own_chip, helper, s)
        slot.append(p * n + sender)
    slot_col = [column(s) for s in slot]
    for k in range(CAP):
        found = jnp.zeros((n, n), jnp.int32)
        for h in (0, 1):
            found += jnp.where(slot_col[h] == lane + k * n, sub + h * n, 0)
        out_ref[TILE_OF + k : TILE_OF + k + 1, :] = jnp.sum(found, axis=0, keepdims=True)

    dst = [dst_ref[h : h + 1, :] for h in (0, 1)]
    key = [d * (2 * n) + lane[0:1] + h * n for h, d in enumerate(dst)]
    key_col = [column(k) for k in key]
    rank = [count(key_col[0] < k) + count(key_col[1] < k) for k in key]
    rank_col = [column(r) for r in rank]
    value_col = [column(s * CHIPS + d) for s, d in zip(slot, dst)]
    for half in (0, 1):
        placed = jnp.zeros((n, n), jnp.int32)
        for h in (0, 1):
            placed += jnp.where(rank_col[h] == lane + half * n, value_col[h], 0)
        out_ref[SEGMENT + half : SEGMENT + half + 1, :] = jnp.sum(placed, axis=0, keepdims=True)
    out_ref[UPTO : UPTO + 1, :] = count(key_col[0] < (lane + 1) * (2 * n)) + count(key_col[1] < (lane + 1) * (2 * n))
    shared_ref[0] = jnp.max(shared)


def exchange_kernel(
    shared, plan, halo_idx, atm_by_field, weights, frac, out_hbm, halo_hbm,
    atm, out_far, out_same, in_far, in_same, lent, borrowed, near, near_out, w_vmem, results, running, fields, rim,
    send_sem, far_sem, same_sem, lend_sem, near_sem, w_sem, rim_send, rim_recv, out_sem,
):
    gx, gy = lax.axis_index("gx"), lax.axis_index("gy")
    myself = gx * 16 + gy
    x, c, y, z = gx // 2, lax.rem(gx, 2), gy // 4, lax.rem(gy, 4)
    other = 1 - c
    far_cap = CAP - 1 if shared else CAP

    def chip_at(i, sign):
        o = lax.rem(i * 37, STEPS) + 1
        cx = lax.rem(x + sign * (o // 16) + 4, 4)
        cy = lax.rem(y + sign * lax.rem(o // 4, 4) + 4, 4)
        cz = lax.rem(z + sign * lax.rem(o, 4) + 4, 4)
        return cx, cy * 4 + cz

    def at(chip, core):
        return chip[0] * 2 + core, chip[1]

    def index(chip, core):
        return chip[0] * 32 + core * 16 + chip[1]

    partner = (x * 2 + other, gy)
    barrier = pltpu.get_barrier_semaphore()
    pl.semaphore_signal(barrier, inc=1, device_id=partner, device_id_type=MESH)

    @pl.loop(0, STEPS)
    def _(i):
        for core in (0, 1):
            pl.semaphore_signal(barrier, inc=1, device_id=at(chip_at(i, 1), core), device_id_type=MESH)

    w_copy = pltpu.make_async_copy(weights, w_vmem, w_sem)
    w_copy.start()

    rows = 16

    @pl.loop(0, atm.shape[0] // rows)
    def _(i):
        part = pl.ds(pl.multiple_of(i * rows, rows), rows)
        atm[part] = jnp.swapaxes(atm_by_field[:, part, :], 0, 1)

    def block(d, k):
        return atm[plan[SEND + k, d]]

    f = atm.shape[1]
    half = atm.shape[2] // 2

    def pack(blocks):
        parts = []
        for b in blocks:
            parts += [b[:, :half], b[:, half:]]
        return jnp.concatenate(parts, axis=0)

    def unpack(buffer, j, k):
        parts = [buffer[j, pl.ds((2 * k + h) * f, f), :] for h in (0, 1)]
        return jnp.concatenate(parts, axis=1)

    if shared:

        @pl.loop(0, CHIPS)
        def _(q):
            lent[q] = block(index((q // 16, lax.rem(q, 16)), other), CAP - 1)

    for k in range(CAP):
        near[CAP + k] = block(myself, k)
        near_out[k] = block(index((x, gy), other), k)
    pl.semaphore_wait(barrier, DEVICES - 1)
    if shared:
        lend = pltpu.make_async_remote_copy(
            src_ref=lent, dst_ref=borrowed, send_sem=lend_sem.at[0], recv_sem=lend_sem.at[1],
            device_id=partner, device_id_type=MESH,
        )
        lend.start()
    near_copy = pltpu.make_async_remote_copy(
        src_ref=near_out, dst_ref=near.at[pl.ds(0, CAP)], send_sem=near_sem.at[0], recv_sem=near_sem.at[1],
        device_id=partner, device_id_type=MESH,
    )

    start = 0
    for g, size in enumerate(FAR_GROUPS):

        @pl.loop(0, size)
        def _(j, g=g, start=start):
            i = start + j
            chip = chip_at(i, 1)
            d = index(chip, other)
            out_far[i] = pack([block(d, k) for k in range(far_cap)])
            pltpu.make_async_remote_copy(
                src_ref=out_far.at[i], dst_ref=in_far[g].at[j],
                send_sem=send_sem.at[0], recv_sem=far_sem.at[g],
                device_id=at(chip, other), device_id_type=MESH,
            ).start()

        start += size

    near_copy.start()
    if shared:
        lend.wait()

    start = 0
    for g, size in enumerate(SAME_GROUPS):

        @pl.loop(0, size)
        def _(j, g=g, start=start):
            i = start + j
            chip = chip_at(i, 1)
            d = index(chip, c)
            blocks = [block(d, k) for k in range(CAP)]
            if shared:
                q = chip[0] * 16 + chip[1]
                blocks[-1] = jnp.where(plan[OWN_THIRD, d] == 1, blocks[-1], borrowed[q])
            out_same[i] = pack(blocks)
            pltpu.make_async_remote_copy(
                src_ref=out_same.at[i], dst_ref=in_same[g].at[j],
                send_sem=send_sem.at[1], recv_sem=same_sem.at[g],
                device_id=at(chip, c), device_id_type=MESH,
            ).start()

        start += size

    w_copy.wait()

    def multiply(s, blocks):
        for k, b in enumerate(blocks):
            results[s + DEVICES * k] = jnp.dot(
                b, w_vmem[plan[TILE_OF + k, s]], preferred_element_type=jnp.float32
            )

    multiply(myself, [near[CAP + k] for k in range(CAP)])
    near_copy.wait()
    multiply(index((x, gy), other), [near[k] for k in range(CAP)])
    for buffers, sems, sizes, core, cap in (
        (in_far, far_sem, FAR_GROUPS, other, far_cap),
        (in_same, same_sem, SAME_GROUPS, c, CAP),
    ):
        start = 0
        for g, size in enumerate(sizes):
            pltpu.make_async_copy(buffers[g], buffers[g], sems.at[g]).wait()

            @pl.loop(0, size)
            def _(j, buffer=buffers[g], start=start, core=core, cap=cap):
                multiply(index(chip_at(start + j, -1), core), [unpack(buffer, j, k) for k in range(cap)])

            start += size

    tiles = running.shape[0]

    def add(r, carry):
        total, previous = carry
        value = plan[SEGMENT + r // DEVICES, lax.rem(r, DEVICES)]
        slot, b = value // CHIPS, lax.rem(value, CHIPS)
        total = total * (b == previous).astype(jnp.float32) + results[slot]
        running[r] = total
        return total, b

    lax.fori_loop(0, tiles, add, (jnp.zeros(running.shape[1:], jnp.float32), jnp.int32(-1)), unroll=8)

    def finished(b):
        upto = plan[UPTO, b]
        before = jnp.where(b > 0, plan[UPTO, jnp.maximum(b - 1, 0)], 0)
        total = jnp.where(upto > before, running[jnp.maximum(upto - 1, 0)], 0.0)
        return (total / frac[pl.ds(b, 1), :]).astype(jnp.bfloat16)

    rim_n = rim.shape[0] // 2
    for side in (0, 1):
        for j in range(rim_n):
            rim[side * rim_n + j] = finished(halo_idx[side, j])
    up, down = lax.rem(myself + 1, DEVICES), lax.rem(myself + DEVICES - 1, DEVICES)
    rim_copies = []
    for side, there in ((1, up), (0, down)):
        copy = pltpu.make_async_remote_copy(
            src_ref=rim.at[pl.ds(side * rim_n, rim_n)],
            dst_ref=halo_hbm.at[1 - side],
            send_sem=rim_send.at[side],
            recv_sem=rim_recv.at[side],
            device_id=(there // 16, lax.rem(there, 16)),
            device_id_type=MESH,
        )
        copy.start()
        rim_copies.append(copy)

    @pl.loop(0, fields.shape[0], unroll=4)
    def _(b):
        fields[b] = finished(b)

    out_copy = pltpu.make_async_copy(fields, out_hbm, out_sem)
    out_copy.start()
    for copy in rim_copies:
        copy.wait()
    out_copy.wait()
    for which, buffer in enumerate((out_far, out_same)):
        pltpu.make_async_copy(buffer, buffer, send_sem.at[which]).wait()


def exchange(shared, plan, halo_idx, atm_by_field, weights, frac):
    tiles, nodes, cells = weights.shape
    fields_n, blocks_n = atm_by_field.shape[:2]
    ocean_n, rim_n = frac.shape[0], halo_idx.shape[1]
    smem = pl.BlockSpec(memory_space=pltpu.SMEM)
    vmem = pl.BlockSpec(memory_space=pltpu.VMEM)
    hbm = pl.BlockSpec(memory_space=pl.ANY)
    far_cap = CAP - 1 if shared else CAP
    lent_n = CHIPS if shared else 1

    def blocks(n):
        return pltpu.VMEM((n, fields_n, nodes), jnp.bfloat16)

    def messages(n, cap):
        return pltpu.VMEM((n, cap * 2 * fields_n, nodes // 2), jnp.bfloat16)

    return pl.pallas_call(
        functools.partial(exchange_kernel, shared),
        out_shape=(
            jax.ShapeDtypeStruct((ocean_n, fields_n, cells), jnp.bfloat16),
            jax.ShapeDtypeStruct((2, rim_n, fields_n, cells), jnp.bfloat16),
        ),
        in_specs=[smem, smem, vmem, hbm, vmem],
        out_specs=(hbm, hbm),
        scratch_shapes=[
            blocks(blocks_n),
            messages(STEPS, far_cap),
            messages(STEPS, CAP),
            [messages(n, far_cap) for n in FAR_GROUPS],
            [messages(n, CAP) for n in SAME_GROUPS],
            blocks(lent_n),
            blocks(lent_n),
            blocks(2 * CAP),
            blocks(CAP),
            pltpu.VMEM(weights.shape, jnp.bfloat16),
            pltpu.VMEM((DEVICES * CAP, fields_n, cells), jnp.float32),
            pltpu.VMEM((tiles, fields_n, cells), jnp.float32),
            pltpu.VMEM((ocean_n, fields_n, cells), jnp.bfloat16),
            pltpu.VMEM((2 * rim_n, fields_n, cells), jnp.bfloat16),
            pltpu.SemaphoreType.DMA((2,)),
            pltpu.SemaphoreType.DMA((len(FAR_GROUPS),)),
            pltpu.SemaphoreType.DMA((len(SAME_GROUPS),)),
            pltpu.SemaphoreType.DMA((2,)),
            pltpu.SemaphoreType.DMA((2,)),
            pltpu.SemaphoreType.DMA,
            pltpu.SemaphoreType.DMA((2,)),
            pltpu.SemaphoreType.DMA((2,)),
            pltpu.SemaphoreType.DMA,
        ],
        compiler_params=pltpu.CompilerParams(
            collective_id=int(shared), has_side_effects=True, vmem_limit_bytes=56 << 20
        ),
        name="remap_shared" if shared else "remap_direct",
    )(plan, halo_idx, atm_by_field, weights, frac)


def per_device(atm_blocks, tile_dev, tile_blk, tile_weights, tile_dst, ocean_frac, halo_send):
    halves = (2 * DEVICES, DEVICES)
    plan, shared = pl.pallas_call(
        plan_kernel,
        out_shape=(jax.ShapeDtypeStruct((ROWS, DEVICES), jnp.int32), jax.ShapeDtypeStruct((1,), jnp.int32)),
        in_specs=[pl.BlockSpec(memory_space=pltpu.VMEM)] * 3,
        out_specs=(pl.BlockSpec(memory_space=pltpu.VMEM), pl.BlockSpec(memory_space=pltpu.SMEM)),
        name="plan",
    )(tile_dev.reshape(halves), tile_blk.reshape(halves), tile_dst.reshape(2, DEVICES))
    fields, halo = lax.cond(
        shared.reshape(()) == 1,
        functools.partial(exchange, True),
        functools.partial(exchange, False),
        plan, halo_send[0], jnp.swapaxes(atm_blocks, 0, 1), tile_weights, ocean_frac,
    )
    return fields, halo[None]


def solution(mesh):
    in_specs = (
        P(("gx", "gy"), None, None),
        P(),
        P(),
        P(("gx", "gy"), None, None),
        P(("gx", "gy")),
        P(("gx", "gy"), None),
        P(("gx", "gy"), None, None),
    )
    out_specs = (P(("gx", "gy"), None, None), P(("gx", "gy"), None, None, None, None))
    return jax.shard_map(
        per_device, mesh=mesh, in_specs=in_specs, out_specs=out_specs, check_vma=False
    )
```

```python
import functools

import jax
import jax.numpy as jnp
from jax import lax
from jax.experimental import pallas as pl
from jax.experimental.pallas import tpu as pltpu
from jax.sharding import PartitionSpec as P

MESH = pl.DeviceIdType.MESH
DEVICES = 128
CHIPS = 64
CAP = 3
STEPS = 63
STRIDE = 29
CORE = 16

SEND, OWN_THIRD, TILE_OF, SEGMENT, UPTO = 0, 3, 4, 7, 9
ROWS = 16


def device_index():
    return lax.axis_index("gx") * 16 + lax.axis_index("gy")


def plan_kernel(dev_ref, blk_ref, dst_ref, out_ref, shared_ref):
    n = DEVICES
    myself = device_index()
    lane = lax.broadcasted_iota(jnp.int32, (n, n), 1)
    sub = lax.broadcasted_iota(jnp.int32, (n, n), 0)
    earlier = sub < lane
    halves = [dev_ref[pl.ds(h, n, stride=2), :] for h in (0, 1)]

    full = jnp.zeros((1, n), jnp.int32)
    columns = [half.T for half in halves]
    chips = [((col >> 5) << 4) | (col & 15) for col in columns]
    units = [jnp.left_shift(1, (chip & 7) * 4) for chip in chips]
    for g in range(CHIPS // 8):
        parts = [jnp.where((chip >> 3) == g, unit, 0) for chip, unit in zip(chips, units)]
        counts = jnp.sum(parts[0] + parts[1], axis=0, keepdims=True)
        for j in range(8):
            full = full | (((counts >> (4 * j)) & 15) == 2 * CAP).astype(jnp.int32)
    shared = 1 - jnp.max(full, axis=1, keepdims=True)

    mine = [(half == myself) for half in halves]
    ones = [m.astype(jnp.float32) for m in mine]
    tri = earlier.astype(jnp.bfloat16)
    nth = [jnp.dot(o.astype(jnp.bfloat16), tri, preferred_element_type=jnp.float32) for o in ones]
    first = jnp.sum(ones[0], axis=1, keepdims=True)
    nth[1] = nth[1] + first
    total = first + jnp.sum(ones[1], axis=1, keepdims=True)
    table = jnp.zeros((n, n), jnp.float32)
    for k in range(CAP):
        picked = jnp.zeros((n, 1), jnp.float32)
        for h in (0, 1):
            blocks = blk_ref[pl.ds(h, n, stride=2), :].astype(jnp.float32)
            picked += jnp.sum(jnp.where(mine[h] & (nth[h] == k), blocks, 0.0), axis=1, keepdims=True)
        table = jnp.where(lane == SEND + k, picked, table)
    table = jnp.where(lane == OWN_THIRD, (total >= CAP).astype(jnp.float32), table)
    out_ref[0:8, :] = table.T[0:8, :].astype(jnp.int32)

    def column(row):
        return jnp.broadcast_to(row, (n, n)).T

    src = [dev_ref[pl.ds(2 * myself + h, 1), :] for h in (0, 1)]
    src_col = [column(s) for s in src]

    def count(mask):
        return jnp.sum(mask.astype(jnp.int32), axis=0, keepdims=True)

    place = [
        count((src_col[0] == src[0]) & earlier),
        count(src_col[0] == src[1]) + count((src_col[1] == src[1]) & earlier),
    ]
    slot = []
    for s, p in zip(src, place):
        helper = (s & ~CORE) | (myself & CORE)
        own_chip = (s & ~CORE) == (myself & ~CORE)
        sender = jnp.where((shared == 1) & (p == CAP - 1) & ~own_chip, helper, s)
        slot.append(p * n + sender)
    slot_col = [column(s) for s in slot]
    for k in range(CAP):
        found = jnp.zeros((n, n), jnp.int32)
        for h in (0, 1):
            found += jnp.where(slot_col[h] == lane + k * n, sub + h * n, 0)
        out_ref[TILE_OF + k : TILE_OF + k + 1, :] = jnp.sum(found, axis=0, keepdims=True)

    dst = [dst_ref[h : h + 1, :] for h in (0, 1)]
    key = [d * (2 * n) + lane[0:1] + h * n for h, d in enumerate(dst)]
    key_col = [column(k) for k in key]
    rank = [count(key_col[0] < k) + count(key_col[1] < k) for k in key]
    rank_col = [column(r) for r in rank]
    value_col = [column(s * CHIPS + d) for s, d in zip(slot, dst)]
    for half in (0, 1):
        placed = jnp.zeros((n, n), jnp.int32)
        for h in (0, 1):
            placed += jnp.where(rank_col[h] == lane + half * n, value_col[h], 0)
        out_ref[SEGMENT + half : SEGMENT + half + 1, :] = jnp.sum(placed, axis=0, keepdims=True)
    out_ref[UPTO : UPTO + 1, :] = count(key_col[0] < (lane + 1) * (2 * n)) + count(key_col[1] < (lane + 1) * (2 * n))
    shared_ref[0] = jnp.max(shared)


def exchange_kernel(
    shared, plan, halo_idx, atm_by_field, weights, frac, out_hbm, halo_hbm,
    atm, out_far, out_same, in_far, in_same, lent, borrowed, near, near_out, w_vmem, results, running, fields, rim,
    send_sem, far_sem, same_sem, lend_sem, near_sem, w_sem, rim_send, rim_recv, out_sem,
):
    gx, gy = lax.axis_index("gx"), lax.axis_index("gy")
    myself = gx * 16 + gy
    x, c, y, z = gx // 2, lax.rem(gx, 2), gy // 4, lax.rem(gy, 4)
    other = 1 - c
    far_cap = CAP - 1 if shared else CAP

    def chip_at(i, sign):
        o = lax.rem(i * STRIDE, STEPS) + 1
        cx = lax.rem(x + sign * (o // 16) + 4, 4)
        cy = lax.rem(y + sign * lax.rem(o // 4, 4) + 4, 4)
        cz = lax.rem(z + sign * lax.rem(o, 4) + 4, 4)
        return cx, cy * 4 + cz

    def at(chip, core):
        return chip[0] * 2 + core, chip[1]

    def index(chip, core):
        return chip[0] * 32 + core * 16 + chip[1]

    partner = (x * 2 + other, gy)
    barrier = pltpu.get_barrier_semaphore()
    pl.semaphore_signal(barrier, inc=1, device_id=partner, device_id_type=MESH)

    @pl.loop(0, STEPS)
    def _(i):
        for core in (0, 1):
            pl.semaphore_signal(barrier, inc=1, device_id=at(chip_at(i, 1), core), device_id_type=MESH)

    w_copy = pltpu.make_async_copy(weights, w_vmem, w_sem)
    w_copy.start()

    rows = 16

    @pl.loop(0, atm.shape[0] // rows)
    def _(i):
        part = pl.ds(pl.multiple_of(i * rows, rows), rows)
        atm[part] = jnp.swapaxes(atm_by_field[:, part, :], 0, 1)

    def block(d, k):
        return atm[plan[SEND + k, d]]

    f = atm.shape[1]
    half = atm.shape[2] // 2

    def pack(blocks):
        parts = []
        for b in blocks:
            parts += [b[:, :half], b[:, half:]]
        return jnp.concatenate(parts, axis=0)

    def unpack(buffer, j, k):
        parts = [buffer[j, pl.ds((2 * k + h) * f, f), :] for h in (0, 1)]
        return jnp.concatenate(parts, axis=1)

    if shared:

        @pl.loop(0, CHIPS)
        def _(q):
            lent[q] = block(index((q // 16, lax.rem(q, 16)), other), CAP - 1)

    for k in range(CAP):
        near[CAP + k] = block(myself, k)
        near_out[k] = block(index((x, gy), other), k)
    pl.semaphore_wait(barrier, DEVICES - 1)
    if shared:
        lend = pltpu.make_async_remote_copy(
            src_ref=lent, dst_ref=borrowed, send_sem=lend_sem.at[0], recv_sem=lend_sem.at[1],
            device_id=partner, device_id_type=MESH,
        )
        lend.start()
    near_copy = pltpu.make_async_remote_copy(
        src_ref=near_out, dst_ref=near.at[pl.ds(0, CAP)], send_sem=near_sem.at[0], recv_sem=near_sem.at[1],
        device_id=partner, device_id_type=MESH,
    )

    def send_far(i):
        chip = chip_at(i, 1)
        d = index(chip, other)
        out_far[i] = pack([block(d, k) for k in range(far_cap)])
        pltpu.make_async_remote_copy(
            src_ref=out_far.at[i], dst_ref=in_far.at[i], send_sem=send_sem.at[0], recv_sem=far_sem.at[i],
            device_id=at(chip, other), device_id_type=MESH,
        ).start()

    def send_same(i):
        chip = chip_at(i, 1)
        d = index(chip, c)
        blocks = [block(d, k) for k in range(CAP)]
        if shared:
            q = chip[0] * 16 + chip[1]
            blocks[-1] = jnp.where(plan[OWN_THIRD, d] == 1, blocks[-1], borrowed[q])
        out_same[i] = pack(blocks)
        pltpu.make_async_remote_copy(
            src_ref=out_same.at[i], dst_ref=in_same.at[i], send_sem=send_sem.at[1], recv_sem=same_sem.at[i],
            device_id=at(chip, c), device_id_type=MESH,
        ).start()

    def multiply(s, blocks):
        for k, b in enumerate(blocks):
            results[s + DEVICES * k] = jnp.dot(
                b, w_vmem[plan[TILE_OF + k, s]], preferred_element_type=jnp.float32
            )

    def wait_far(i):
        pltpu.make_async_copy(in_far.at[i], in_far.at[i], far_sem.at[i]).wait()

    def wait_same(i):
        pltpu.make_async_copy(in_same.at[i], in_same.at[i], same_sem.at[i]).wait()

    def take_far(i):
        multiply(index(chip_at(i, -1), other), [unpack(in_far, i, k) for k in range(far_cap)])

    def take_same(i):
        multiply(index(chip_at(i, -1), c), [unpack(in_same, i, k) for k in range(CAP)])

    @pl.loop(0, STEPS)
    def _(i):
        send_far(i)

    near_copy.start()
    if shared:
        lend.wait()

    @pl.loop(0, STEPS)
    def _(i):
        send_same(i)

    w_copy.wait()
    multiply(myself, [near[CAP + k] for k in range(CAP)])
    near_copy.wait()
    multiply(index((x, gy), other), [near[k] for k in range(CAP)])

    @pl.loop(0, STEPS // 7)
    def _(g):
        for j in range(7):
            wait_far(g * 7 + j)
        for j in range(7):
            take_far(g * 7 + j)

    @pl.loop(0, STEPS // 7)
    def _(g):
        for j in range(7):
            wait_same(g * 7 + j)
        for j in range(7):
            take_same(g * 7 + j)

    middle = running.shape[0] // 2

    def add(r, carry):
        new = []
        for (total, previous), at_r in zip(carry, (r, r + middle)):
            value = plan[SEGMENT + at_r // DEVICES, lax.rem(at_r, DEVICES)]
            slot, b = value // CHIPS, lax.rem(value, CHIPS)
            total = jnp.where(b == previous, total, 0.0) + results[slot]
            running[at_r] = total
            new.append((total, b))
        return tuple(new)

    none = (jnp.zeros(running.shape[1:], jnp.float32), jnp.int32(-1))
    lax.fori_loop(0, middle, add, (none, none), unroll=4)

    def finished(b):
        upto = plan[UPTO, b]
        before = jnp.where(b > 0, plan[UPTO, jnp.maximum(b - 1, 0)], 0)
        total = jnp.where(upto > before, running[jnp.maximum(upto - 1, 0)], 0.0)
        total += jnp.where((before < middle) & (upto > middle), running[middle - 1], 0.0)
        return total / frac[pl.ds(b, 1), :]

    def by_field(blocks):
        return jnp.swapaxes(jnp.stack(blocks), 0, 1).astype(jnp.bfloat16)

    rim_n = rim.shape[2]
    for side in (0, 1):
        rim[side] = by_field([finished(halo_idx[side, j]) for j in range(rim_n)])
    up, down = lax.rem(myself + 1, DEVICES), lax.rem(myself + DEVICES - 1, DEVICES)
    rim_copies = []
    for side, there in ((1, up), (0, down)):
        copy = pltpu.make_async_remote_copy(
            src_ref=rim.at[side],
            dst_ref=halo_hbm.at[1 - side],
            send_sem=rim_send.at[side],
            recv_sem=rim_recv.at[side],
            device_id=(there // 16, lax.rem(there, 16)),
            device_id_type=MESH,
        )
        copy.start()
        rim_copies.append(copy)

    @pl.loop(0, fields.shape[1] // rows)
    def _(i):
        first = pl.multiple_of(i * rows, rows)
        fields[:, pl.ds(first, rows), :] = by_field([finished(first + j) for j in range(rows)])

    out_copy = pltpu.make_async_copy(fields, out_hbm, out_sem)
    out_copy.start()
    for copy in rim_copies:
        copy.wait()
    out_copy.wait()
    for which, buffer in enumerate((out_far, out_same)):
        pltpu.make_async_copy(buffer, buffer, send_sem.at[which]).wait()


def exchange(shared, plan, halo_idx, atm_by_field, weights, frac):
    tiles, nodes, cells = weights.shape
    fields_n, blocks_n = atm_by_field.shape[:2]
    ocean_n, rim_n = frac.shape[0], halo_idx.shape[1]
    smem = pl.BlockSpec(memory_space=pltpu.SMEM)
    vmem = pl.BlockSpec(memory_space=pltpu.VMEM)
    hbm = pl.BlockSpec(memory_space=pl.ANY)
    far_cap = CAP - 1 if shared else CAP
    lent_n = CHIPS if shared else 1

    def blocks(n):
        return pltpu.VMEM((n, fields_n, nodes), jnp.bfloat16)

    def messages(n, cap):
        return pltpu.VMEM((n, cap * 2 * fields_n, nodes // 2), jnp.bfloat16)

    return pl.pallas_call(
        functools.partial(exchange_kernel, shared),
        out_shape=(
            jax.ShapeDtypeStruct((fields_n, ocean_n, cells), jnp.bfloat16),
            jax.ShapeDtypeStruct((2, fields_n, rim_n, cells), jnp.bfloat16),
        ),
        in_specs=[smem, smem, vmem, hbm, vmem],
        out_specs=(hbm, hbm),
        scratch_shapes=[
            blocks(blocks_n),
            messages(STEPS, far_cap),
            messages(STEPS, CAP),
            messages(STEPS, far_cap),
            messages(STEPS, CAP),
            blocks(lent_n),
            blocks(lent_n),
            blocks(2 * CAP),
            blocks(CAP),
            pltpu.VMEM(weights.shape, jnp.bfloat16),
            pltpu.VMEM((DEVICES * CAP, fields_n, cells), jnp.float32),
            pltpu.VMEM((tiles, fields_n, cells), jnp.float32),
            pltpu.VMEM((fields_n, ocean_n, cells), jnp.bfloat16),
            pltpu.VMEM((2, fields_n, rim_n, cells), jnp.bfloat16),
            pltpu.SemaphoreType.DMA((2,)),
            pltpu.SemaphoreType.DMA((STEPS,)),
            pltpu.SemaphoreType.DMA((STEPS,)),
            pltpu.SemaphoreType.DMA((2,)),
            pltpu.SemaphoreType.DMA((2,)),
            pltpu.SemaphoreType.DMA,
            pltpu.SemaphoreType.DMA((2,)),
            pltpu.SemaphoreType.DMA((2,)),
            pltpu.SemaphoreType.DMA,
        ],
        compiler_params=pltpu.CompilerParams(
            collective_id=int(shared), has_side_effects=True, vmem_limit_bytes=56 << 20
        ),
        name="remap_shared" if shared else "remap_direct",
    )(plan, halo_idx, atm_by_field, weights, frac)


def per_device(atm_blocks, tile_dev, tile_blk, tile_weights, tile_dst, ocean_frac, halo_send):
    halves = (2 * DEVICES, DEVICES)
    plan, shared = pl.pallas_call(
        plan_kernel,
        out_shape=(jax.ShapeDtypeStruct((ROWS, DEVICES), jnp.int32), jax.ShapeDtypeStruct((1,), jnp.int32)),
        in_specs=[pl.BlockSpec(memory_space=pltpu.VMEM)] * 3,
        out_specs=(pl.BlockSpec(memory_space=pltpu.VMEM), pl.BlockSpec(memory_space=pltpu.SMEM)),
        name="plan",
    )(tile_dev.reshape(halves), tile_blk.reshape(halves), tile_dst.reshape(2, DEVICES))
    fields, halo = lax.cond(
        shared.reshape(()) == 1,
        functools.partial(exchange, True),
        functools.partial(exchange, False),
        plan, halo_send[0], jnp.swapaxes(atm_blocks, 0, 1), tile_weights, ocean_frac,
    )
    return jnp.swapaxes(fields, 0, 1), jnp.swapaxes(halo, 1, 2)[None]


def solution(mesh):
    in_specs = (
        P(("gx", "gy"), None, None),
        P(),
        P(),
        P(("gx", "gy"), None, None),
        P(("gx", "gy")),
        P(("gx", "gy"), None),
        P(("gx", "gy"), None, None),
    )
    out_specs = (P(("gx", "gy"), None, None), P(("gx", "gy"), None, None, None, None))
    return jax.shard_map(
        per_device, mesh=mesh, in_specs=in_specs, out_specs=out_specs, check_vma=False
    )
```

```python
import functools

import jax
import jax.numpy as jnp
from jax import lax
from jax.experimental import pallas as pl
from jax.experimental.pallas import tpu as pltpu
from jax.sharding import PartitionSpec as P

MESH = pl.DeviceIdType.MESH
DEVICES = 128
CHIPS = 64
CAP = 3
STEPS = 63
STRIDE = 29
CORE = 16

SEND, OWN_THIRD, TILE_OF, SEGMENT, UPTO = 0, 3, 4, 7, 9
ROWS = 16


def device_index():
    return lax.axis_index("gx") * 16 + lax.axis_index("gy")


def plan_kernel(dev_ref, blk_ref, dst_ref, out_ref, shared_ref):
    n = DEVICES
    myself = device_index()
    lane = lax.broadcasted_iota(jnp.int32, (n, n), 1)
    sub = lax.broadcasted_iota(jnp.int32, (n, n), 0)
    earlier = sub < lane
    halves = [dev_ref[pl.ds(h, n, stride=2), :] for h in (0, 1)]

    full = jnp.zeros((1, n), jnp.int32)
    columns = [half.T for half in halves]
    chips = [((col >> 5) << 4) | (col & 15) for col in columns]
    units = [jnp.left_shift(1, (chip & 7) * 4) for chip in chips]
    for g in range(CHIPS // 8):
        parts = [jnp.where((chip >> 3) == g, unit, 0) for chip, unit in zip(chips, units)]
        counts = jnp.sum(parts[0] + parts[1], axis=0, keepdims=True)
        for j in range(8):
            full = full | (((counts >> (4 * j)) & 15) == 2 * CAP).astype(jnp.int32)
    shared = 1 - jnp.max(full, axis=1, keepdims=True)

    mine = [(half == myself) for half in halves]
    ones = [m.astype(jnp.float32) for m in mine]
    tri = earlier.astype(jnp.bfloat16)
    nth = [jnp.dot(o.astype(jnp.bfloat16), tri, preferred_element_type=jnp.float32) for o in ones]
    first = jnp.sum(ones[0], axis=1, keepdims=True)
    nth[1] = nth[1] + first
    total = first + jnp.sum(ones[1], axis=1, keepdims=True)
    table = jnp.zeros((n, n), jnp.float32)
    for k in range(CAP):
        picked = jnp.zeros((n, 1), jnp.float32)
        for h in (0, 1):
            blocks = blk_ref[pl.ds(h, n, stride=2), :].astype(jnp.float32)
            picked += jnp.sum(jnp.where(mine[h] & (nth[h] == k), blocks, 0.0), axis=1, keepdims=True)
        table = jnp.where(lane == SEND + k, picked, table)
    table = jnp.where(lane == OWN_THIRD, (total >= CAP).astype(jnp.float32), table)
    out_ref[0:8, :] = table.T[0:8, :].astype(jnp.int32)

    def column(row):
        return jnp.broadcast_to(row, (n, n)).T

    src = [dev_ref[pl.ds(2 * myself + h, 1), :] for h in (0, 1)]
    src_col = [column(s) for s in src]

    def count(mask):
        return jnp.sum(mask.astype(jnp.int32), axis=0, keepdims=True)

    place = [
        count((src_col[0] == src[0]) & earlier),
        count(src_col[0] == src[1]) + count((src_col[1] == src[1]) & earlier),
    ]
    slot = []
    for s, p in zip(src, place):
        helper = (s & ~CORE) | (myself & CORE)
        own_chip = (s & ~CORE) == (myself & ~CORE)
        sender = jnp.where((shared == 1) & (p == CAP - 1) & ~own_chip, helper, s)
        slot.append(p * n + sender)
    slot_col = [column(s) for s in slot]
    for k in range(CAP):
        found = jnp.zeros((n, n), jnp.int32)
        for h in (0, 1):
            found += jnp.where(slot_col[h] == lane + k * n, sub + h * n, 0)
        out_ref[TILE_OF + k : TILE_OF + k + 1, :] = jnp.sum(found, axis=0, keepdims=True)

    dst = [dst_ref[h : h + 1, :] for h in (0, 1)]
    key = [d * (2 * n) + lane[0:1] + h * n for h, d in enumerate(dst)]
    key_col = [column(k) for k in key]
    rank = [count(key_col[0] < k) + count(key_col[1] < k) for k in key]
    rank_col = [column(r) for r in rank]
    value_col = [column(s * CHIPS + d) for s, d in zip(slot, dst)]
    for half in (0, 1):
        placed = jnp.zeros((n, n), jnp.int32)
        for h in (0, 1):
            placed += jnp.where(rank_col[h] == lane + half * n, value_col[h], 0)
        out_ref[SEGMENT + half : SEGMENT + half + 1, :] = jnp.sum(placed, axis=0, keepdims=True)
    out_ref[UPTO : UPTO + 1, :] = count(key_col[0] < (lane + 1) * (2 * n)) + count(key_col[1] < (lane + 1) * (2 * n))
    shared_ref[0] = jnp.max(shared)


def exchange_kernel(
    shared, plan, halo_idx, atm_by_field, weights, frac, out_hbm, halo_hbm,
    atm, out_far, out_same, in_far, in_same, lent, borrowed, near, near_out, w_vmem, results, running, fields, rim,
    send_sem, far_sem, same_sem, lend_sem, near_sem, w_sem, rim_send, rim_recv, out_sem,
):
    gx, gy = lax.axis_index("gx"), lax.axis_index("gy")
    myself = gx * 16 + gy
    x, c, y, z = gx // 2, lax.rem(gx, 2), gy // 4, lax.rem(gy, 4)
    other = 1 - c
    far_cap = CAP - 1 if shared else CAP

    def chip_at(i, sign):
        o = lax.rem(i * STRIDE, STEPS) + 1
        cx = lax.rem(x + sign * (o // 16) + 4, 4)
        cy = lax.rem(y + sign * lax.rem(o // 4, 4) + 4, 4)
        cz = lax.rem(z + sign * lax.rem(o, 4) + 4, 4)
        return cx, cy * 4 + cz

    def at(chip, core):
        return chip[0] * 2 + core, chip[1]

    def index(chip, core):
        return chip[0] * 32 + core * 16 + chip[1]

    partner = (x * 2 + other, gy)
    barrier = pltpu.get_barrier_semaphore()
    pl.semaphore_signal(barrier, inc=1, device_id=partner, device_id_type=MESH)

    @pl.loop(0, STEPS)
    def _(i):
        for core in (0, 1):
            pl.semaphore_signal(barrier, inc=1, device_id=at(chip_at(i, 1), core), device_id_type=MESH)

    w_copy = pltpu.make_async_copy(weights, w_vmem, w_sem)
    w_copy.start()

    rows = 16

    @pl.loop(0, atm.shape[0] // rows)
    def _(i):
        part = pl.ds(pl.multiple_of(i * rows, rows), rows)
        atm[part] = jnp.swapaxes(atm_by_field[:, part, :], 0, 1)

    def block(d, k):
        return atm[plan[SEND + k, d]]

    f = atm.shape[1]
    half = atm.shape[2] // 2

    def pack(blocks):
        parts = []
        for b in blocks:
            parts += [b[:, :half], b[:, half:]]
        return jnp.concatenate(parts, axis=0)

    def unpack(buffer, j, k):
        parts = [buffer[j, pl.ds((2 * k + h) * f, f), :] for h in (0, 1)]
        return jnp.concatenate(parts, axis=1)

    if shared:

        @pl.loop(0, CHIPS)
        def _(q):
            lent[q] = block(index((q // 16, lax.rem(q, 16)), other), CAP - 1)

    for k in range(CAP):
        near[CAP + k] = block(myself, k)
        near_out[k] = block(index((x, gy), other), k)
    pl.semaphore_wait(barrier, DEVICES - 1)
    if shared:
        lend = pltpu.make_async_remote_copy(
            src_ref=lent, dst_ref=borrowed, send_sem=lend_sem.at[0], recv_sem=lend_sem.at[1],
            device_id=partner, device_id_type=MESH,
        )
        lend.start()
    near_copy = pltpu.make_async_remote_copy(
        src_ref=near_out, dst_ref=near.at[pl.ds(0, CAP)], send_sem=near_sem.at[0], recv_sem=near_sem.at[1],
        device_id=partner, device_id_type=MESH,
    )

    def send_far(i):
        chip = chip_at(i, 1)
        d = index(chip, other)
        out_far[i] = pack([block(d, k) for k in range(far_cap)])
        pltpu.make_async_remote_copy(
            src_ref=out_far.at[i], dst_ref=in_far.at[i], send_sem=send_sem.at[0], recv_sem=far_sem.at[i],
            device_id=at(chip, other), device_id_type=MESH,
        ).start()

    def send_same(i):
        chip = chip_at(i, 1)
        d = index(chip, c)
        blocks = [block(d, k) for k in range(CAP)]
        if shared:
            q = chip[0] * 16 + chip[1]
            blocks[-1] = jnp.where(plan[OWN_THIRD, d] == 1, blocks[-1], borrowed[q])
        out_same[i] = pack(blocks)
        pltpu.make_async_remote_copy(
            src_ref=out_same.at[i], dst_ref=in_same.at[i], send_sem=send_sem.at[1], recv_sem=same_sem.at[i],
            device_id=at(chip, c), device_id_type=MESH,
        ).start()

    def multiply(s, blocks):
        for k, b in enumerate(blocks):
            results[s + DEVICES * k] = jnp.dot(
                b, w_vmem[plan[TILE_OF + k, s]], preferred_element_type=jnp.float32
            )

    def wait_far(i):
        pltpu.make_async_copy(in_far.at[i], in_far.at[i], far_sem.at[i]).wait()

    def wait_same(i):
        pltpu.make_async_copy(in_same.at[i], in_same.at[i], same_sem.at[i]).wait()

    def take_far(i):
        multiply(index(chip_at(i, -1), other), [unpack(in_far, i, k) for k in range(far_cap)])

    def take_same(i):
        multiply(index(chip_at(i, -1), c), [unpack(in_same, i, k) for k in range(CAP)])

    @pl.loop(0, STEPS)
    def _(i):
        send_far(i)

    near_copy.start()
    if shared:
        lend.wait()

    @pl.loop(0, STEPS)
    def _(i):
        send_same(i)

    w_copy.wait()
    multiply(myself, [near[CAP + k] for k in range(CAP)])
    near_copy.wait()
    multiply(index((x, gy), other), [near[k] for k in range(CAP)])

    @pl.loop(0, STEPS // 7)
    def _(g):
        for j in range(7):
            wait_far(g * 7 + j)
        for j in range(7):
            take_far(g * 7 + j)

    @pl.loop(0, STEPS // 7)
    def _(g):
        for j in range(7):
            wait_same(g * 7 + j)
        for j in range(7):
            take_same(g * 7 + j)

    middle = running.shape[0] // 2

    def add(r, carry):
        new = []
        for h, (total, previous) in enumerate(carry):
            value = plan[SEGMENT + h, r]
            b = value & (CHIPS - 1)
            total = jnp.where(b == previous, total, 0.0) + results[value >> 6]
            running[h * middle + r] = total
            new.append((total, b))
        return tuple(new)

    none = (jnp.zeros(running.shape[1:], jnp.float32), jnp.int32(-1))
    lax.fori_loop(0, middle, add, (none, none), unroll=8)

    def finished(b):
        upto = plan[UPTO, b]
        before = jnp.where(b > 0, plan[UPTO, jnp.maximum(b - 1, 0)], 0)
        total = jnp.where(upto > before, running[jnp.maximum(upto - 1, 0)], 0.0)
        total += jnp.where((before < middle) & (upto > middle), running[middle - 1], 0.0)
        return total / frac[pl.ds(b, 1), :]

    def by_field(blocks):
        return jnp.swapaxes(jnp.stack(blocks), 0, 1).astype(jnp.bfloat16)

    rim_n = rim.shape[2]
    for side in (0, 1):
        rim[side] = by_field([finished(halo_idx[side, j]) for j in range(rim_n)])
    up, down = lax.rem(myself + 1, DEVICES), lax.rem(myself + DEVICES - 1, DEVICES)
    rim_copies = []
    for side, there in ((1, up), (0, down)):
        copy = pltpu.make_async_remote_copy(
            src_ref=rim.at[side],
            dst_ref=halo_hbm.at[1 - side],
            send_sem=rim_send.at[side],
            recv_sem=rim_recv.at[side],
            device_id=(there // 16, lax.rem(there, 16)),
            device_id_type=MESH,
        )
        copy.start()
        rim_copies.append(copy)

    @pl.loop(0, fields.shape[1] // rows)
    def _(i):
        first = pl.multiple_of(i * rows, rows)
        fields[:, pl.ds(first, rows), :] = by_field([finished(first + j) for j in range(rows)])

    out_copy = pltpu.make_async_copy(fields, out_hbm, out_sem)
    out_copy.start()
    for copy in rim_copies:
        copy.wait()
    out_copy.wait()
    for which, buffer in enumerate((out_far, out_same)):
        pltpu.make_async_copy(buffer, buffer, send_sem.at[which]).wait()


def exchange(shared, plan, halo_idx, atm_by_field, weights, frac):
    tiles, nodes, cells = weights.shape
    fields_n, blocks_n = atm_by_field.shape[:2]
    ocean_n, rim_n = frac.shape[0], halo_idx.shape[1]
    smem = pl.BlockSpec(memory_space=pltpu.SMEM)
    vmem = pl.BlockSpec(memory_space=pltpu.VMEM)
    hbm = pl.BlockSpec(memory_space=pl.ANY)
    far_cap = CAP - 1 if shared else CAP
    lent_n = CHIPS if shared else 1

    def blocks(n):
        return pltpu.VMEM((n, fields_n, nodes), jnp.bfloat16)

    def messages(n, cap):
        return pltpu.VMEM((n, cap * 2 * fields_n, nodes // 2), jnp.bfloat16)

    return pl.pallas_call(
        functools.partial(exchange_kernel, shared),
        out_shape=(
            jax.ShapeDtypeStruct((fields_n, ocean_n, cells), jnp.bfloat16),
            jax.ShapeDtypeStruct((2, fields_n, rim_n, cells), jnp.bfloat16),
        ),
        in_specs=[smem, smem, vmem, hbm, vmem],
        out_specs=(hbm, hbm),
        scratch_shapes=[
            blocks(blocks_n),
            messages(STEPS, far_cap),
            messages(STEPS, CAP),
            messages(STEPS, far_cap),
            messages(STEPS, CAP),
            blocks(lent_n),
            blocks(lent_n),
            blocks(2 * CAP),
            blocks(CAP),
            pltpu.VMEM(weights.shape, jnp.bfloat16),
            pltpu.VMEM((DEVICES * CAP, fields_n, cells), jnp.float32),
            pltpu.VMEM((tiles, fields_n, cells), jnp.float32),
            pltpu.VMEM((fields_n, ocean_n, cells), jnp.bfloat16),
            pltpu.VMEM((2, fields_n, rim_n, cells), jnp.bfloat16),
            pltpu.SemaphoreType.DMA((2,)),
            pltpu.SemaphoreType.DMA((STEPS,)),
            pltpu.SemaphoreType.DMA((STEPS,)),
            pltpu.SemaphoreType.DMA((2,)),
            pltpu.SemaphoreType.DMA((2,)),
            pltpu.SemaphoreType.DMA,
            pltpu.SemaphoreType.DMA((2,)),
            pltpu.SemaphoreType.DMA((2,)),
            pltpu.SemaphoreType.DMA,
        ],
        compiler_params=pltpu.CompilerParams(
            collective_id=int(shared), has_side_effects=True, vmem_limit_bytes=56 << 20
        ),
        name="remap_shared" if shared else "remap_direct",
    )(plan, halo_idx, atm_by_field, weights, frac)


def per_device(atm_blocks, tile_dev, tile_blk, tile_weights, tile_dst, ocean_frac, halo_send):
    halves = (2 * DEVICES, DEVICES)
    plan, shared = pl.pallas_call(
        plan_kernel,
        out_shape=(jax.ShapeDtypeStruct((ROWS, DEVICES), jnp.int32), jax.ShapeDtypeStruct((1,), jnp.int32)),
        in_specs=[pl.BlockSpec(memory_space=pltpu.VMEM)] * 3,
        out_specs=(pl.BlockSpec(memory_space=pltpu.VMEM), pl.BlockSpec(memory_space=pltpu.SMEM)),
        name="plan",
    )(tile_dev.reshape(halves), tile_blk.reshape(halves), tile_dst.reshape(2, DEVICES))
    fields, halo = lax.cond(
        shared.reshape(()) == 1,
        functools.partial(exchange, True),
        functools.partial(exchange, False),
        plan, halo_send[0], jnp.swapaxes(atm_blocks, 0, 1), tile_weights, ocean_frac,
    )
    return jnp.swapaxes(fields, 0, 1), jnp.swapaxes(halo, 1, 2)[None]


def solution(mesh):
    in_specs = (
        P(("gx", "gy"), None, None),
        P(),
        P(),
        P(("gx", "gy"), None, None),
        P(("gx", "gy")),
        P(("gx", "gy"), None),
        P(("gx", "gy"), None, None),
    )
    out_specs = (P(("gx", "gy"), None, None), P(("gx", "gy"), None, None, None, None))
    return jax.shard_map(
        per_device, mesh=mesh, in_specs=in_specs, out_specs=out_specs, check_vma=False
    )
```

```python
import functools

import jax
import jax.numpy as jnp
from jax import lax
from jax.experimental import pallas as pl
from jax.experimental.pallas import tpu as pltpu
from jax.sharding import PartitionSpec as P

MESH = pl.DeviceIdType.MESH
DEVICES = 128
CHIPS = 64
CAP = 3
STEPS = 63
STRIDE = 29
CORE = 16

SEND, OWN_THIRD, TILE_OF, SEGMENT, UPTO = 0, 3, 4, 7, 9
ROWS = 16


def device_index():
    return lax.axis_index("gx") * 16 + lax.axis_index("gy")


def plan_kernel(dev_ref, blk_ref, dst_ref, out_ref, shared_ref):
    n = DEVICES
    myself = device_index()
    lane = lax.broadcasted_iota(jnp.int32, (n, n), 1)
    sub = lax.broadcasted_iota(jnp.int32, (n, n), 0)
    earlier = sub < lane
    halves = [dev_ref[pl.ds(h, n, stride=2), :] for h in (0, 1)]

    full = jnp.zeros((1, n), jnp.int32)
    columns = [half.T for half in halves]
    chips = [((col >> 5) << 4) | (col & 15) for col in columns]
    units = [jnp.left_shift(1, (chip & 7) * 4) for chip in chips]
    for g in range(CHIPS // 8):
        parts = [jnp.where((chip >> 3) == g, unit, 0) for chip, unit in zip(chips, units)]
        counts = jnp.sum(parts[0] + parts[1], axis=0, keepdims=True)
        for j in range(8):
            full = full | (((counts >> (4 * j)) & 15) == 2 * CAP).astype(jnp.int32)
    shared = 1 - jnp.max(full, axis=1, keepdims=True)

    mine = [(half == myself) for half in halves]
    ones = [m.astype(jnp.float32) for m in mine]
    tri = earlier.astype(jnp.bfloat16)
    nth = [jnp.dot(o.astype(jnp.bfloat16), tri, preferred_element_type=jnp.float32) for o in ones]
    first = jnp.sum(ones[0], axis=1, keepdims=True)
    nth[1] = nth[1] + first
    total = first + jnp.sum(ones[1], axis=1, keepdims=True)
    table = jnp.zeros((n, n), jnp.float32)
    for k in range(CAP):
        picked = jnp.zeros((n, 1), jnp.float32)
        for h in (0, 1):
            blocks = blk_ref[pl.ds(h, n, stride=2), :].astype(jnp.float32)
            picked += jnp.sum(jnp.where(mine[h] & (nth[h] == k), blocks, 0.0), axis=1, keepdims=True)
        table = jnp.where(lane == SEND + k, picked, table)
    table = jnp.where(lane == OWN_THIRD, (total >= CAP).astype(jnp.float32), table)
    out_ref[0:8, :] = table.T[0:8, :].astype(jnp.int32)

    def column(row):
        return jnp.broadcast_to(row, (n, n)).T

    src = [dev_ref[pl.ds(2 * myself + h, 1), :] for h in (0, 1)]
    src_col = [column(s) for s in src]

    def count(mask):
        return jnp.sum(mask.astype(jnp.int32), axis=0, keepdims=True)

    place = [
        count((src_col[0] == src[0]) & earlier),
        count(src_col[0] == src[1]) + count((src_col[1] == src[1]) & earlier),
    ]
    slot = []
    for s, p in zip(src, place):
        helper = (s & ~CORE) | (myself & CORE)
        own_chip = (s & ~CORE) == (myself & ~CORE)
        sender = jnp.where((shared == 1) & (p == CAP - 1) & ~own_chip, helper, s)
        slot.append(p * n + sender)
    slot_col = [column(s) for s in slot]
    for k in range(CAP):
        found = jnp.zeros((n, n), jnp.int32)
        for h in (0, 1):
            found += jnp.where(slot_col[h] == lane + k * n, sub + h * n, 0)
        out_ref[TILE_OF + k : TILE_OF + k + 1, :] = jnp.sum(found, axis=0, keepdims=True)

    dst = [dst_ref[h : h + 1, :] for h in (0, 1)]
    key = [d * (2 * n) + lane[0:1] + h * n for h, d in enumerate(dst)]
    key_col = [column(k) for k in key]
    rank = [count(key_col[0] < k) + count(key_col[1] < k) for k in key]
    rank_col = [column(r) for r in rank]
    value_col = [column(s * CHIPS + d) for s, d in zip(slot, dst)]
    for half in (0, 1):
        placed = jnp.zeros((n, n), jnp.int32)
        for h in (0, 1):
            placed += jnp.where(rank_col[h] == lane + half * n, value_col[h], 0)
        out_ref[SEGMENT + half : SEGMENT + half + 1, :] = jnp.sum(placed, axis=0, keepdims=True)
    out_ref[UPTO : UPTO + 1, :] = count(key_col[0] < (lane + 1) * (2 * n)) + count(key_col[1] < (lane + 1) * (2 * n))
    shared_ref[0] = jnp.max(shared)


def exchange_kernel(
    shared, plan, halo_idx, atm_hbm, weights, frac_hbm, out_hbm, halo_hbm,
    atm_by_field, frac, input_sem, atm, out_far, out_same, in_far, in_same, lent, borrowed, near, near_out, w_vmem, results, running, fields, rim,
    send_sem, far_sem, same_sem, lend_sem, near_sem, w_sem, rim_send, rim_recv, out_sem,
):
    gx, gy = lax.axis_index("gx"), lax.axis_index("gy")
    myself = gx * 16 + gy
    x, c, y, z = gx // 2, lax.rem(gx, 2), gy // 4, lax.rem(gy, 4)
    other = 1 - c
    far_cap = CAP - 1 if shared else CAP

    def chip_at(i, sign):
        o = lax.rem(i * STRIDE, STEPS) + 1
        cx = lax.rem(x + sign * (o // 16) + 4, 4)
        cy = lax.rem(y + sign * lax.rem(o // 4, 4) + 4, 4)
        cz = lax.rem(z + sign * lax.rem(o, 4) + 4, 4)
        return cx, cy * 4 + cz

    def at(chip, core):
        return chip[0] * 2 + core, chip[1]

    def index(chip, core):
        return chip[0] * 32 + core * 16 + chip[1]

    atm_copy = pltpu.make_async_copy(atm_hbm, atm_by_field, input_sem.at[0])
    atm_copy.start()
    frac_copy = pltpu.make_async_copy(frac_hbm, frac, input_sem.at[1])
    frac_copy.start()
    partner = (x * 2 + other, gy)
    barrier = pltpu.get_barrier_semaphore()
    pl.semaphore_signal(barrier, inc=1, device_id=partner, device_id_type=MESH)

    @pl.loop(0, STEPS)
    def _(i):
        for core in (0, 1):
            pl.semaphore_signal(barrier, inc=1, device_id=at(chip_at(i, 1 - 2 * c), core), device_id_type=MESH)

    w_copy = pltpu.make_async_copy(weights, w_vmem, w_sem)
    w_copy.start()

    atm_copy.wait()
    rows = 16

    @pl.loop(0, atm.shape[0] // rows)
    def _(i):
        part = pl.ds(pl.multiple_of(i * rows, rows), rows)
        atm[part] = jnp.swapaxes(atm_by_field[:, part, :], 0, 1)

    def block(d, k):
        return atm[plan[SEND + k, d]]

    f = atm.shape[1]
    half = atm.shape[2] // 2

    def pack(blocks):
        parts = []
        for b in blocks:
            parts += [b[:, :half], b[:, half:]]
        return jnp.concatenate(parts, axis=0)

    def unpack(buffer, j, k):
        parts = [buffer[j, pl.ds((2 * k + h) * f, f), :] for h in (0, 1)]
        return jnp.concatenate(parts, axis=1)

    if shared:

        @pl.loop(0, CHIPS)
        def _(q):
            lent[q] = block(index((q // 16, lax.rem(q, 16)), other), CAP - 1)

    for k in range(CAP):
        near[CAP + k] = block(myself, k)
        near_out[k] = block(index((x, gy), other), k)
    pl.semaphore_wait(barrier, DEVICES - 1)
    if shared:
        lend = pltpu.make_async_remote_copy(
            src_ref=lent, dst_ref=borrowed, send_sem=lend_sem.at[0], recv_sem=lend_sem.at[1],
            device_id=partner, device_id_type=MESH,
        )
        lend.start()
    near_copy = pltpu.make_async_remote_copy(
        src_ref=near_out, dst_ref=near.at[pl.ds(0, CAP)], send_sem=near_sem.at[0], recv_sem=near_sem.at[1],
        device_id=partner, device_id_type=MESH,
    )

    def send_far(i):
        chip = chip_at(i, 1 - 2 * c)
        d = index(chip, other)
        out_far[i] = pack([block(d, k) for k in range(far_cap)])
        pltpu.make_async_remote_copy(
            src_ref=out_far.at[i], dst_ref=in_far.at[i], send_sem=send_sem.at[0], recv_sem=far_sem.at[i],
            device_id=at(chip, other), device_id_type=MESH,
        ).start()

    def send_same(i):
        chip = chip_at(i, 1 - 2 * c)
        d = index(chip, c)
        blocks = [block(d, k) for k in range(CAP)]
        if shared:
            q = chip[0] * 16 + chip[1]
            blocks[-1] = jnp.where(plan[OWN_THIRD, d] == 1, blocks[-1], borrowed[q])
        out_same[i] = pack(blocks)
        pltpu.make_async_remote_copy(
            src_ref=out_same.at[i], dst_ref=in_same.at[i], send_sem=send_sem.at[1], recv_sem=same_sem.at[i],
            device_id=at(chip, c), device_id_type=MESH,
        ).start()

    def multiply(s, blocks):
        for k, b in enumerate(blocks):
            results[s + DEVICES * k] = jnp.dot(
                b, w_vmem[plan[TILE_OF + k, s]], preferred_element_type=jnp.float32
            )

    def wait_far(i):
        pltpu.make_async_copy(in_far.at[i], in_far.at[i], far_sem.at[i]).wait()

    def wait_same(i):
        pltpu.make_async_copy(in_same.at[i], in_same.at[i], same_sem.at[i]).wait()

    def take_far(i):
        multiply(index(chip_at(i, 1 - 2 * c), other), [unpack(in_far, i, k) for k in range(far_cap)])

    def take_same(i):
        multiply(index(chip_at(i, 2 * c - 1), c), [unpack(in_same, i, k) for k in range(CAP)])

    @pl.loop(0, STEPS)
    def _(i):
        send_far(i)

    near_copy.start()
    if shared:
        lend.wait()

    @pl.loop(0, STEPS)
    def _(i):
        send_same(i)

    frac_copy.wait()
    w_copy.wait()
    multiply(myself, [near[CAP + k] for k in range(CAP)])
    near_copy.wait()
    multiply(index((x, gy), other), [near[k] for k in range(CAP)])

    @pl.loop(0, STEPS // 7)
    def _(g):
        for j in range(7):
            wait_far(g * 7 + j)
        for j in range(7):
            take_far(g * 7 + j)

    @pl.loop(0, STEPS // 7)
    def _(g):
        for j in range(7):
            wait_same(g * 7 + j)
        for j in range(7):
            take_same(g * 7 + j)

    middle = running.shape[0] // 2

    def add(r, carry):
        new = []
        for h, (total, previous) in enumerate(carry):
            value = plan[SEGMENT + h, r]
            b = value & (CHIPS - 1)
            total = jnp.where(b == previous, total, 0.0) + results[value >> 6]
            running[h * middle + r] = total
            new.append((total, b))
        return tuple(new)

    none = (jnp.zeros(running.shape[1:], jnp.float32), jnp.int32(-1))
    lax.fori_loop(0, middle, add, (none, none), unroll=8)

    def finished(b):
        upto = plan[UPTO, b]
        before = jnp.where(b > 0, plan[UPTO, jnp.maximum(b - 1, 0)], 0)
        total = jnp.where(upto > before, running[jnp.maximum(upto - 1, 0)], 0.0)
        total += jnp.where((before < middle) & (upto > middle), running[middle - 1], 0.0)
        return total / frac[pl.ds(b, 1), :]

    def by_field(blocks):
        return jnp.swapaxes(jnp.stack(blocks), 0, 1).astype(jnp.bfloat16)

    rim_n = rim.shape[2]
    up, down = lax.rem(myself + 1, DEVICES), lax.rem(myself + DEVICES - 1, DEVICES)
    rim_copies = []
    for side, there in ((1, up), (0, down)):
        rim[side] = by_field([finished(halo_idx[side, j]) for j in range(rim_n)])
        copy = pltpu.make_async_remote_copy(
            src_ref=rim.at[side],
            dst_ref=halo_hbm.at[1 - side],
            send_sem=rim_send.at[side],
            recv_sem=rim_recv.at[side],
            device_id=(there // 16, lax.rem(there, 16)),
            device_id_type=MESH,
        )
        copy.start()
        rim_copies.append(copy)

    @pl.loop(0, fields.shape[1] // rows)
    def _(i):
        first = pl.multiple_of(i * rows, rows)
        fields[:, pl.ds(first, rows), :] = by_field([finished(first + j) for j in range(rows)])

    out_copy = pltpu.make_async_copy(fields, out_hbm, out_sem)
    out_copy.start()
    for copy in rim_copies:
        copy.wait()
    out_copy.wait()
    for which, buffer in enumerate((out_far, out_same)):
        pltpu.make_async_copy(buffer, buffer, send_sem.at[which]).wait()


def exchange(shared, plan, halo_idx, atm_by_field, weights, frac):
    tiles, nodes, cells = weights.shape
    fields_n, blocks_n = atm_by_field.shape[:2]
    ocean_n, rim_n = frac.shape[0], halo_idx.shape[1]
    smem = pl.BlockSpec(memory_space=pltpu.SMEM)
    hbm = pl.BlockSpec(memory_space=pl.ANY)
    far_cap = CAP - 1 if shared else CAP
    lent_n = CHIPS if shared else 1

    def blocks(n):
        return pltpu.VMEM((n, fields_n, nodes), jnp.bfloat16)

    def messages(n, cap):
        return pltpu.VMEM((n, cap * 2 * fields_n, nodes // 2), jnp.bfloat16)

    return pl.pallas_call(
        functools.partial(exchange_kernel, shared),
        out_shape=(
            jax.ShapeDtypeStruct((fields_n, ocean_n, cells), jnp.bfloat16),
            jax.ShapeDtypeStruct((2, fields_n, rim_n, cells), jnp.bfloat16),
        ),
        in_specs=[smem, smem, hbm, hbm, hbm],
        out_specs=(hbm, hbm),
        scratch_shapes=[
            pltpu.VMEM(atm_by_field.shape, jnp.bfloat16),
            pltpu.VMEM(frac.shape, jnp.float32),
            pltpu.SemaphoreType.DMA((2,)),
            blocks(blocks_n),
            messages(STEPS, far_cap),
            messages(STEPS, CAP),
            messages(STEPS, far_cap),
            messages(STEPS, CAP),
            blocks(lent_n),
            blocks(lent_n),
            blocks(2 * CAP),
            blocks(CAP),
            pltpu.VMEM(weights.shape, jnp.bfloat16),
            pltpu.VMEM((DEVICES * CAP, fields_n, cells), jnp.float32),
            pltpu.VMEM((tiles, fields_n, cells), jnp.float32),
            pltpu.VMEM((fields_n, ocean_n, cells), jnp.bfloat16),
            pltpu.VMEM((2, fields_n, rim_n, cells), jnp.bfloat16),
            pltpu.SemaphoreType.DMA((2,)),
            pltpu.SemaphoreType.DMA((STEPS,)),
            pltpu.SemaphoreType.DMA((STEPS,)),
            pltpu.SemaphoreType.DMA((2,)),
            pltpu.SemaphoreType.DMA((2,)),
            pltpu.SemaphoreType.DMA,
            pltpu.SemaphoreType.DMA((2,)),
            pltpu.SemaphoreType.DMA((2,)),
            pltpu.SemaphoreType.DMA,
        ],
        compiler_params=pltpu.CompilerParams(
            collective_id=int(shared), has_side_effects=True, vmem_limit_bytes=56 << 20
        ),
        name="remap_shared" if shared else "remap_direct",
    )(plan, halo_idx, atm_by_field, weights, frac)


def per_device(atm_blocks, tile_dev, tile_blk, tile_weights, tile_dst, ocean_frac, halo_send):
    halves = (2 * DEVICES, DEVICES)
    plan, shared = pl.pallas_call(
        plan_kernel,
        out_shape=(jax.ShapeDtypeStruct((ROWS, DEVICES), jnp.int32), jax.ShapeDtypeStruct((1,), jnp.int32)),
        in_specs=[pl.BlockSpec(memory_space=pltpu.VMEM)] * 3,
        out_specs=(pl.BlockSpec(memory_space=pltpu.VMEM), pl.BlockSpec(memory_space=pltpu.SMEM)),
        name="plan",
    )(tile_dev.reshape(halves), tile_blk.reshape(halves), tile_dst.reshape(2, DEVICES))
    fields, halo = lax.cond(
        shared.reshape(()) == 1,
        functools.partial(exchange, True),
        functools.partial(exchange, False),
        plan, halo_send[0], jnp.swapaxes(atm_blocks, 0, 1), tile_weights, ocean_frac,
    )
    return jnp.swapaxes(fields, 0, 1), jnp.swapaxes(halo, 1, 2)[None]


def solution(mesh):
    in_specs = (
        P(("gx", "gy"), None, None),
        P(),
        P(),
        P(("gx", "gy"), None, None),
        P(("gx", "gy")),
        P(("gx", "gy"), None),
        P(("gx", "gy"), None, None),
    )
    out_specs = (P(("gx", "gy"), None, None), P(("gx", "gy"), None, None, None, None))
    return jax.shard_map(
        per_device, mesh=mesh, in_specs=in_specs, out_specs=out_specs, check_vma=False
    )
```

```python
import functools

import jax
import jax.numpy as jnp
from jax import lax
from jax.experimental import pallas as pl
from jax.experimental.pallas import tpu as pltpu
from jax.sharding import PartitionSpec as P

MESH = pl.DeviceIdType.MESH
DEVICES = 128
CHIPS = 64
CAP = 3
STEPS = 63
STRIDE = 29
CORE = 16

SEND, OWN_THIRD, TILE_OF, SEGMENT, UPTO = 0, 3, 4, 7, 9
ROWS = 16


def device_index():
    return lax.axis_index("gx") * 16 + lax.axis_index("gy")


def plan_kernel(dev_ref, blk_ref, dst_ref, out_ref, shared_ref):
    n = DEVICES
    myself = device_index()
    lane = lax.broadcasted_iota(jnp.int32, (n, n), 1)
    sub = lax.broadcasted_iota(jnp.int32, (n, n), 0)
    earlier = sub < lane
    halves = [dev_ref[pl.ds(h, n, stride=2), :] for h in (0, 1)]

    full = jnp.zeros((1, n), jnp.int32)
    columns = [half.T for half in halves]
    chips = [((col >> 5) << 4) | (col & 15) for col in columns]
    units = [jnp.left_shift(1, (chip & 7) * 4) for chip in chips]
    for g in range(CHIPS // 8):
        parts = [jnp.where((chip >> 3) == g, unit, 0) for chip, unit in zip(chips, units)]
        counts = jnp.sum(parts[0] + parts[1], axis=0, keepdims=True)
        for j in range(8):
            full = full | (((counts >> (4 * j)) & 15) == 2 * CAP).astype(jnp.int32)
    shared = 1 - jnp.max(full, axis=1, keepdims=True)

    mine = [(half == myself) for half in halves]
    ones = [m.astype(jnp.float32) for m in mine]
    tri = earlier.astype(jnp.bfloat16)
    nth = [jnp.dot(o.astype(jnp.bfloat16), tri, preferred_element_type=jnp.float32) for o in ones]
    first = jnp.sum(ones[0], axis=1, keepdims=True)
    nth[1] = nth[1] + first
    total = first + jnp.sum(ones[1], axis=1, keepdims=True)
    table = jnp.zeros((n, n), jnp.float32)
    for k in range(CAP):
        picked = jnp.zeros((n, 1), jnp.float32)
        for h in (0, 1):
            blocks = blk_ref[pl.ds(h, n, stride=2), :].astype(jnp.float32)
            picked += jnp.sum(jnp.where(mine[h] & (nth[h] == k), blocks, 0.0), axis=1, keepdims=True)
        table = jnp.where(lane == SEND + k, picked, table)
    table = jnp.where(lane == OWN_THIRD, (total >= CAP).astype(jnp.float32), table)
    out_ref[0:8, :] = table.T[0:8, :].astype(jnp.int32)

    def column(row):
        return jnp.broadcast_to(row, (n, n)).T

    src = [dev_ref[pl.ds(2 * myself + h, 1), :] for h in (0, 1)]
    src_col = [column(s) for s in src]

    def count(mask):
        return jnp.sum(mask.astype(jnp.int32), axis=0, keepdims=True)

    place = [
        count((src_col[0] == src[0]) & earlier),
        count(src_col[0] == src[1]) + count((src_col[1] == src[1]) & earlier),
    ]
    slot = []
    for s, p in zip(src, place):
        helper = (s & ~CORE) | (myself & CORE)
        own_chip = (s & ~CORE) == (myself & ~CORE)
        sender = jnp.where((shared == 1) & (p == CAP - 1) & ~own_chip, helper, s)
        slot.append(p * n + sender)
    slot_col = [column(s) for s in slot]
    for k in range(CAP):
        found = jnp.zeros((n, n), jnp.int32)
        for h in (0, 1):
            found += jnp.where(slot_col[h] == lane + k * n, sub + h * n, 0)
        out_ref[TILE_OF + k : TILE_OF + k + 1, :] = jnp.sum(found, axis=0, keepdims=True)

    dst = [dst_ref[h : h + 1, :] for h in (0, 1)]
    key = [d * (2 * n) + lane[0:1] + h * n for h, d in enumerate(dst)]
    key_col = [column(k) for k in key]
    rank = [count(key_col[0] < k) + count(key_col[1] < k) for k in key]
    rank_col = [column(r) for r in rank]
    value_col = [column(s * CHIPS + d) for s, d in zip(slot, dst)]
    for half in (0, 1):
        placed = jnp.zeros((n, n), jnp.int32)
        for h in (0, 1):
            placed += jnp.where(rank_col[h] == lane + half * n, value_col[h], 0)
        out_ref[SEGMENT + half : SEGMENT + half + 1, :] = jnp.sum(placed, axis=0, keepdims=True)
    out_ref[UPTO : UPTO + 1, :] = count(key_col[0] < (lane + 1) * (2 * n)) + count(key_col[1] < (lane + 1) * (2 * n))
    shared_ref[0] = jnp.max(shared)


def exchange_kernel(
    shared, plan, halo_idx, atm_hbm, weights, frac_hbm, out_hbm, halo_hbm,
    atm_by_field, frac, input_sem, atm, out_far, out_same, in_far, in_same, lent, borrowed, near, near_out, w_vmem, results, running, fields, rim,
    send_sem, far_sem, same_sem, lend_sem, near_sem, w_sem, rim_send, rim_recv, out_sem,
):
    gx, gy = lax.axis_index("gx"), lax.axis_index("gy")
    myself = gx * 16 + gy
    x, c, y, z = gx // 2, lax.rem(gx, 2), gy // 4, lax.rem(gy, 4)
    other = 1 - c
    far_cap = CAP - 1 if shared else CAP

    def chip_at(i, sign):
        o = lax.rem(i * STRIDE, STEPS) + 1
        cx = lax.rem(x + sign * (o // 16) + 4, 4)
        cy = lax.rem(y + sign * lax.rem(o // 4, 4) + 4, 4)
        cz = lax.rem(z + sign * lax.rem(o, 4) + 4, 4)
        return cx, cy * 4 + cz

    def at(chip, core):
        return chip[0] * 2 + core, chip[1]

    def index(chip, core):
        return chip[0] * 32 + core * 16 + chip[1]

    atm_copy = pltpu.make_async_copy(atm_hbm, atm_by_field, input_sem.at[0])
    atm_copy.start()
    frac_copy = pltpu.make_async_copy(frac_hbm, frac, input_sem.at[1])
    frac_copy.start()
    partner = (x * 2 + other, gy)
    barrier = pltpu.get_barrier_semaphore()
    def greet(ahead):
        there = lax.rem(myself + ahead, DEVICES)
        device = (there // 16, lax.rem(there, 16))
        pl.semaphore_signal(barrier, inc=1, device_id=device, device_id_type=MESH)

    greet(DEVICES - 1)

    @pl.loop(0, (DEVICES - 2) // 7)
    def _(i):
        for j in range(7):
            greet(i * 7 + j + 1)

    w_copy = pltpu.make_async_copy(weights, w_vmem, w_sem)
    w_copy.start()

    atm_copy.wait()
    rows = 16

    @pl.loop(0, atm.shape[0] // rows)
    def _(i):
        part = pl.ds(pl.multiple_of(i * rows, rows), rows)
        atm[part] = jnp.swapaxes(atm_by_field[:, part, :], 0, 1)

    def block(d, k):
        return atm[plan[SEND + k, d]]

    f = atm.shape[1]
    half = atm.shape[2] // 2

    def pack(blocks):
        parts = []
        for b in blocks:
            parts += [b[:, :half], b[:, half:]]
        return jnp.concatenate(parts, axis=0)

    def unpack(buffer, j, k):
        parts = [buffer[j, pl.ds((2 * k + h) * f, f), :] for h in (0, 1)]
        return jnp.concatenate(parts, axis=1)

    if shared:

        @pl.loop(0, CHIPS)
        def _(q):
            lent[q] = block(index((q // 16, lax.rem(q, 16)), other), CAP - 1)

    for k in range(CAP):
        near[CAP + k] = block(myself, k)
        near_out[k] = block(index((x, gy), other), k)
    pl.semaphore_wait(barrier, DEVICES - 1)
    if shared:
        lend = pltpu.make_async_remote_copy(
            src_ref=lent, dst_ref=borrowed, send_sem=lend_sem.at[0], recv_sem=lend_sem.at[1],
            device_id=partner, device_id_type=MESH,
        )
        lend.start()
    near_copy = pltpu.make_async_remote_copy(
        src_ref=near_out, dst_ref=near.at[pl.ds(0, CAP)], send_sem=near_sem.at[0], recv_sem=near_sem.at[1],
        device_id=partner, device_id_type=MESH,
    )

    def send_far(i):
        chip = chip_at(i, 1 - 2 * c)
        d = index(chip, other)
        out_far[i] = pack([block(d, k) for k in range(far_cap)])
        pltpu.make_async_remote_copy(
            src_ref=out_far.at[i], dst_ref=in_far.at[i], send_sem=send_sem.at[0], recv_sem=far_sem.at[i],
            device_id=at(chip, other), device_id_type=MESH,
        ).start()

    def send_same(i):
        chip = chip_at(i, 1 - 2 * c)
        d = index(chip, c)
        blocks = [block(d, k) for k in range(CAP)]
        if shared:
            q = chip[0] * 16 + chip[1]
            blocks[-1] = jnp.where(plan[OWN_THIRD, d] == 1, blocks[-1], borrowed[q])
        out_same[i] = pack(blocks)
        pltpu.make_async_remote_copy(
            src_ref=out_same.at[i], dst_ref=in_same.at[i], send_sem=send_sem.at[1], recv_sem=same_sem.at[i],
            device_id=at(chip, c), device_id_type=MESH,
        ).start()

    def multiply(s, blocks):
        for k, b in enumerate(blocks):
            results[s + DEVICES * k] = jnp.dot(
                b, w_vmem[plan[TILE_OF + k, s]], preferred_element_type=jnp.float32
            )

    def wait_far(i):
        pltpu.make_async_copy(in_far.at[i], in_far.at[i], far_sem.at[i]).wait()

    def wait_same(i):
        pltpu.make_async_copy(in_same.at[i], in_same.at[i], same_sem.at[i]).wait()

    def take_far(i):
        multiply(index(chip_at(i, 1 - 2 * c), other), [unpack(in_far, i, k) for k in range(far_cap)])

    def take_same(i):
        multiply(index(chip_at(i, 2 * c - 1), c), [unpack(in_same, i, k) for k in range(CAP)])

    @pl.loop(0, STEPS)
    def _(i):
        send_far(i)

    near_copy.start()
    if shared:
        lend.wait()

    @pl.loop(0, STEPS)
    def _(i):
        send_same(i)

    frac_copy.wait()
    w_copy.wait()
    multiply(myself, [near[CAP + k] for k in range(CAP)])
    near_copy.wait()
    multiply(index((x, gy), other), [near[k] for k in range(CAP)])

    @pl.loop(0, STEPS // 7)
    def _(g):
        for j in range(7):
            wait_far(g * 7 + j)
        for j in range(7):
            take_far(g * 7 + j)

    @pl.loop(0, STEPS // 7)
    def _(g):
        for j in range(7):
            wait_same(g * 7 + j)
        for j in range(7):
            take_same(g * 7 + j)

    middle = running.shape[0] // 2

    def add(r, carry):
        new = []
        for h, (total, previous) in enumerate(carry):
            value = plan[SEGMENT + h, r]
            b = value & (CHIPS - 1)
            total = jnp.where(b == previous, total, 0.0) + results[value >> 6]
            running[h * middle + r] = total
            new.append((total, b))
        return tuple(new)

    none = (jnp.zeros(running.shape[1:], jnp.float32), jnp.int32(-1))
    lax.fori_loop(0, middle, add, (none, none), unroll=8)

    def finished(b):
        upto = plan[UPTO, b]
        before = jnp.where(b > 0, plan[UPTO, jnp.maximum(b - 1, 0)], 0)
        total = jnp.where(upto > before, running[jnp.maximum(upto - 1, 0)], 0.0)
        total += jnp.where((before < middle) & (upto > middle), running[middle - 1], 0.0)
        return total / frac[pl.ds(b, 1), :]

    def by_field(blocks):
        return jnp.swapaxes(jnp.stack(blocks), 0, 1).astype(jnp.bfloat16)

    rim_n = rim.shape[2]
    up, down = lax.rem(myself + 1, DEVICES), lax.rem(myself + DEVICES - 1, DEVICES)
    rim_copies = []
    for side, there in ((1, up), (0, down)):
        rim[side] = by_field([finished(halo_idx[side, j]) for j in range(rim_n)])
        copy = pltpu.make_async_remote_copy(
            src_ref=rim.at[side],
            dst_ref=halo_hbm.at[1 - side],
            send_sem=rim_send.at[side],
            recv_sem=rim_recv.at[side],
            device_id=(there // 16, lax.rem(there, 16)),
            device_id_type=MESH,
        )
        copy.start()
        rim_copies.append(copy)

    @pl.loop(0, fields.shape[1] // rows)
    def _(i):
        first = pl.multiple_of(i * rows, rows)
        fields[:, pl.ds(first, rows), :] = by_field([finished(first + j) for j in range(rows)])

    out_copy = pltpu.make_async_copy(fields, out_hbm, out_sem)
    out_copy.start()
    for copy in rim_copies:
        copy.wait()
    out_copy.wait()
    for which, buffer in enumerate((out_far, out_same)):
        pltpu.make_async_copy(buffer, buffer, send_sem.at[which]).wait()


def exchange(shared, plan, halo_idx, atm_by_field, weights, frac):
    tiles, nodes, cells = weights.shape
    fields_n, blocks_n = atm_by_field.shape[:2]
    ocean_n, rim_n = frac.shape[0], halo_idx.shape[1]
    smem = pl.BlockSpec(memory_space=pltpu.SMEM)
    hbm = pl.BlockSpec(memory_space=pl.ANY)
    far_cap = CAP - 1 if shared else CAP
    lent_n = CHIPS if shared else 1

    def blocks(n):
        return pltpu.VMEM((n, fields_n, nodes), jnp.bfloat16)

    def messages(n, cap):
        return pltpu.VMEM((n, cap * 2 * fields_n, nodes // 2), jnp.bfloat16)

    return pl.pallas_call(
        functools.partial(exchange_kernel, shared),
        out_shape=(
            jax.ShapeDtypeStruct((fields_n, ocean_n, cells), jnp.bfloat16),
            jax.ShapeDtypeStruct((2, fields_n, rim_n, cells), jnp.bfloat16),
        ),
        in_specs=[smem, smem, hbm, hbm, hbm],
        out_specs=(hbm, hbm),
        scratch_shapes=[
            pltpu.VMEM(atm_by_field.shape, jnp.bfloat16),
            pltpu.VMEM(frac.shape, jnp.float32),
            pltpu.SemaphoreType.DMA((2,)),
            blocks(blocks_n),
            messages(STEPS, far_cap),
            messages(STEPS, CAP),
            messages(STEPS, far_cap),
            messages(STEPS, CAP),
            blocks(lent_n),
            blocks(lent_n),
            blocks(2 * CAP),
            blocks(CAP),
            pltpu.VMEM(weights.shape, jnp.bfloat16),
            pltpu.VMEM((DEVICES * CAP, fields_n, cells), jnp.float32),
            pltpu.VMEM((tiles, fields_n, cells), jnp.float32),
            pltpu.VMEM((fields_n, ocean_n, cells), jnp.bfloat16),
            pltpu.VMEM((2, fields_n, rim_n, cells), jnp.bfloat16),
            pltpu.SemaphoreType.DMA((2,)),
            pltpu.SemaphoreType.DMA((STEPS,)),
            pltpu.SemaphoreType.DMA((STEPS,)),
            pltpu.SemaphoreType.DMA((2,)),
            pltpu.SemaphoreType.DMA((2,)),
            pltpu.SemaphoreType.DMA,
            pltpu.SemaphoreType.DMA((2,)),
            pltpu.SemaphoreType.DMA((2,)),
            pltpu.SemaphoreType.DMA,
        ],
        compiler_params=pltpu.CompilerParams(
            collective_id=int(shared), has_side_effects=True, vmem_limit_bytes=56 << 20
        ),
        name="remap_shared" if shared else "remap_direct",
    )(plan, halo_idx, atm_by_field, weights, frac)


def per_device(atm_blocks, tile_dev, tile_blk, tile_weights, tile_dst, ocean_frac, halo_send):
    halves = (2 * DEVICES, DEVICES)
    plan, shared = pl.pallas_call(
        plan_kernel,
        out_shape=(jax.ShapeDtypeStruct((ROWS, DEVICES), jnp.int32), jax.ShapeDtypeStruct((1,), jnp.int32)),
        in_specs=[pl.BlockSpec(memory_space=pltpu.VMEM)] * 3,
        out_specs=(pl.BlockSpec(memory_space=pltpu.VMEM), pl.BlockSpec(memory_space=pltpu.SMEM)),
        name="plan",
    )(tile_dev.reshape(halves), tile_blk.reshape(halves), tile_dst.reshape(2, DEVICES))
    fields, halo = lax.cond(
        shared.reshape(()) == 1,
        functools.partial(exchange, True),
        functools.partial(exchange, False),
        plan, halo_send[0], jnp.swapaxes(atm_blocks, 0, 1), tile_weights, ocean_frac,
    )
    return jnp.swapaxes(fields, 0, 1), jnp.swapaxes(halo, 1, 2)[None]


def solution(mesh):
    in_specs = (
        P(("gx", "gy"), None, None),
        P(),
        P(),
        P(("gx", "gy"), None, None),
        P(("gx", "gy")),
        P(("gx", "gy"), None),
        P(("gx", "gy"), None, None),
    )
    out_specs = (P(("gx", "gy"), None, None), P(("gx", "gy"), None, None, None, None))
    return jax.shard_map(
        per_device, mesh=mesh, in_specs=in_specs, out_specs=out_specs, check_vma=False
    )
```
